32 devices in a mesh: dp: 8 (over z, y), mp: 4 (over x, core).
Axes of the slice: x: 2, y: 2, z: 4, core: 2. Of those that a mesh axis runs over, the one named last changes fastest.
Arguments:
- dec_in: bfloat16 [2, 512, 768], P(None, 'dp'), may hold values from -6 to 6
- encoded: bfloat16 [2, 98304, 768], P(None, 'dp'), may hold values from -6 to 6
- seg_lengths: int32 [2, 8, 64], P(None, 'dp'), may hold values from 1 to 512, 12288 in all within a row
- pair_slot: int32 [2, 512], replicated, may hold values from 0 to 511, as said below
- relevance: float32 [2, 512], P(None, 'dp'), may hold values from -6 to 6
- score_dir: bfloat16 [768], replicated, may hold values from -0.21875 to 0.21875
- gain_self: bfloat16 [768], P('dp'), may hold values from 0.5 to 1.5
- gain_cross: bfloat16 [768], P('dp'), may hold values from 0.5 to 1.5
- gain_ff: bfloat16 [768], P('dp'), may hold values from 0.5 to 1.5
- self_value: bfloat16 [768, 768], P('dp', 'mp'), may hold values from -0.21875 to 0.21875
- self_out: bfloat16 [768, 768], P('mp', 'dp'), may hold values from -0.21875 to 0.21875
- cross_query: bfloat16 [768, 768], P('dp', 'mp'), may hold values from -0.0546875 to 0.0546875
- cross_key: bfloat16 [768, 768], P('dp', 'mp'), may hold values from -0.21875 to 0.21875
- cross_value: bfloat16 [768, 768], P('dp', 'mp'), may hold values from -0.21875 to 0.21875
- cross_out: bfloat16 [768, 768], P('mp', 'dp'), may hold values from -1.25 to 1.25
- ff_in: bfloat16 [768, 3072], P('dp', 'mp'), may hold values from -0.21875 to 0.21875
- ff_out: bfloat16 [3072, 768], P('mp', 'dp'), may hold values from -0.109375 to 0.109375
Outputs:
- dec_out: float32 [2, 512, 768], P(None, 'dp')
- d_dec_in: float32 [2, 512, 768], P(None, 'dp')
- d_encoded: bfloat16 [2, 98304, 768], P(None, ('dp', 'mp'))
- g_gain_self: float32 [768], P('dp')
- g_gain_cross: float32 [768], P('dp')
- g_gain_ff: float32 [768], P('dp')
- g_self_value: float32 [768, 768], P('dp', 'mp')
- g_self_out: float32 [768, 768], P('mp', 'dp')
- g_cross_query: float32 [768, 768], P('dp', 'mp')
- g_cross_key: float32 [768, 768], P('dp', 'mp')
- g_cross_value: float32 [768, 768], P('dp', 'mp')
- g_cross_out: float32 [768, 768], P('mp', 'dp')
- g_ff_in: float32 [768, 3072], P('dp', 'mp')
- g_ff_out: float32 [3072, 768], P('mp', 'dp')
The draws below stay inside these ranges and needn't reach their ends.
Inputs may be any that keep to these rules, and one draw needn't show every extreme that they name: `seg_lengths`: each row holds the segment lengths of the 64 pairs of one index of dp in one micro-batch; a row sums to 12288 and its largest entry is 512. `pair_slot`: for each micro-batch a permutation of the 512 pairs onto slots; slot r belongs to query r // 16 and to index r // 64 of dp; of the 64 pairs of each index of dp exactly 8 go to slots of each index.
All inputs are finite; a program needn't handle non-finite values.
Results may differ from the reference program's by a relative error of at most 0.04.
Values may be sent and summed in bfloat16 or wider, within the bound.
A program may use at most 256 MiB of HBM per device.

```python
import math
import jax
import jax.numpy as jnp
import numpy as np
from jax import lax

D = 768
HEADS = 12
HEAD_DIM = 64
FF = 3072
TOK_MB = 12288
PAIRS_MB = 64
CAND = 16
SEG_MAX = 512
MICRO = 2
ENC_TOKENS = 98304
PAIRS_ALL = 512
PER_PEER = 8
N_DP = 8


def draw_pair_slot(key, part):
    key = jax.random.fold_in(key, 7)
    first, second = jax.random.split(key)
    device_count = PAIRS_ALL // PAIRS_MB
    row_count = MICRO * device_count
    ranking = jax.vmap(lambda sub_key: jax.random.permutation(sub_key, PAIRS_MB))(jax.random.split(first, row_count))
    spread = jax.vmap(lambda sub_key: jax.random.permutation(sub_key, PAIRS_MB))(jax.random.split(second, row_count))
    ranking = ranking.reshape(MICRO, device_count, PAIRS_MB).astype(jnp.int32)
    spread = spread.reshape(MICRO, device_count * PAIRS_MB).astype(jnp.int32)
    source = jnp.arange(device_count, dtype=jnp.int32)[None, :, None]
    target = ranking // PER_PEER
    arrive = source * PER_PEER + ranking % PER_PEER
    within = jnp.take_along_axis(spread, (target * PAIRS_MB + arrive).reshape(MICRO, -1), axis=1)
    slot_ids = target.reshape(MICRO, -1) * PAIRS_MB + within
    return slot_ids.astype(jnp.int32)


def level_of(key, dims, shards, low, top_value):
    gain = 1.0
    for axis_at, parts in shards:
        steps = jax.random.uniform(jax.random.fold_in(jax.random.fold_in(key, 6), axis_at), (parts,), jnp.float32, low / len(shards), top_value / len(shards))
        gain = gain * jnp.repeat(jnp.exp(steps), dims[axis_at] // parts).reshape((-1,) + (1,) * (len(dims) - 1 - axis_at))
    return gain


def length_profile(number_of, total, most, slope):
    portions = [(1 << 20) // math.isqrt(rank ** slope) + 1 for rank in range(2, number_of + 1)]
    surplus, holding = total - most - (number_of - 1), [1] * (number_of - 1)
    while surplus > 0:
        candidates = [i for i in range(number_of - 1) if holding[i] < most]
        mass, budget = sum([portions[i] for i in candidates]), surplus
        for i in candidates:
            addition = min(most - holding[i], max(1, budget * portions[i] // mass), surplus)
            holding[i] = holding[i] + addition
            surplus = surplus - addition
    return np.array([most] + holding)


def ragged_sizes(own_key, count, total, limit, lean):
    if count == 2:
        one = jax.random.randint(own_key, (), max(1, total - limit), min(limit, total - 1) + 1)
        return jnp.stack([one, total - one])
    sizes = jnp.asarray(length_profile(count, total, limit, lean), jnp.int32)
    twos = (count - 1) // 2
    donor, sink = sizes[1:1 + 2 * twos:2], sizes[2:2 + 2 * twos:2]
    room = jnp.minimum(donor - 1, limit - sink)
    moved = jax.random.randint(jax.random.fold_in(own_key, 1), (twos,), 0, 1 << 20) % (room + 1)
    sizes = sizes.at[1:1 + 2 * twos:2].set(donor - moved).at[2:2 + 2 * twos:2].set(sink + moved)
    return sizes[jax.random.permutation(jax.random.fold_in(own_key, 2), count)]


def normal_values(key, dims, deviation, limit, cuts=(), kind=jnp.bfloat16):
    values = deviation * jax.random.normal(key, dims, jnp.float32)
    if cuts:
        values = values * level_of(key, dims, cuts, -0.22, 0.18)
    return jnp.clip(values, -limit, limit).astype(kind)


def setup_inputs(seed: int = 0) -> dict:
    arg_keys = jax.random.split(jax.random.key(seed), 18)
    return {
        "dec_in": normal_values(arg_keys[0], (MICRO, PAIRS_ALL, D), 1.0, 6.0, ((1, 8),)),
        "encoded": normal_values(arg_keys[1], (MICRO, ENC_TOKENS, D), 1.0, 6.0, ((1, 8),)),
        "seg_lengths": jax.vmap(lambda own: ragged_sizes(own, PAIRS_MB, TOK_MB, SEG_MAX, 2))(jax.random.split(arg_keys[2], MICRO * N_DP)).reshape((MICRO, N_DP, PAIRS_MB)).astype(jnp.int32),
        "pair_slot": draw_pair_slot(jax.random.fold_in(arg_keys[17], 71), 0),
        "relevance": normal_values(arg_keys[4], (MICRO, PAIRS_ALL), 1.5, 6.0, ((1, 8),), jnp.float32),
        "score_dir": normal_values(arg_keys[5], (D,), D ** -0.5, 0.21875),
        "gain_self": jnp.clip(1.0 + 0.1 * jax.random.normal(arg_keys[6], (D,), jnp.float32), 0.5, 1.5).astype(jnp.bfloat16),
        "gain_cross": jnp.clip(1.0 + 0.1 * jax.random.normal(arg_keys[7], (D,), jnp.float32), 0.5, 1.5).astype(jnp.bfloat16),
        "gain_ff": jnp.clip(1.0 + 0.1 * jax.random.normal(arg_keys[8], (D,), jnp.float32), 0.5, 1.5).astype(jnp.bfloat16),
        "self_value": normal_values(arg_keys[9], (D, D), D ** -0.5, 0.21875, ((0, 8), (1, 4))),
        "self_out": normal_values(arg_keys[10], (D, D), D ** -0.5, 0.21875, ((0, 4), (1, 8))),
        "cross_query": normal_values(arg_keys[11], (D, D), (16 * D) ** -0.5, 0.0546875, ((0, 8), (1, 4))),
        "cross_key": normal_values(arg_keys[12], (D, D), D ** -0.5, 0.21875, ((0, 8), (1, 4))),
        "cross_value": normal_values(arg_keys[13], (D, D), D ** -0.5, 0.21875, ((0, 8), (1, 4))),
        "cross_out": normal_values(arg_keys[14], (D, D), (D // 32) ** -0.5, 1.25, ((0, 4), (1, 8))),
        "ff_in": normal_values(arg_keys[15], (D, FF), D ** -0.5, 0.21875, ((0, 8), (1, 4))),
        "ff_out": normal_values(arg_keys[16], (FF, D), FF ** -0.5, 0.109375, ((0, 4), (1, 8))),
    }


@jax.custom_vjp
def low(v):
    return lax.optimization_barrier(v.astype(jnp.bfloat16)).astype(jnp.float32)

@jax.custom_vjp
def low_back(v):
    return v

def low_keep(v):
    return (low(v), None)

def low_pass(kept, grad):
    return (grad,)

def back_keep(v):
    return (v, None)

def back_low(kept, grad):
    return (low(grad),)
low.defvjp(low_keep, low_pass)
low_back.defvjp(back_keep, back_low)
norm_eps = 1e-06

def rms_norm(values, gain_row):
    return values * lax.rsqrt(lax.optimization_barrier(jnp.mean(values * values, axis=-1, keepdims=True)) + norm_eps) * gain_row

def project(values, weight):
    return low_back(jnp.dot(low(values), weight, precision=lax.Precision.HIGHEST))

def group_layer(weights, stream_in, encoder_rows, lengths):
    gain_self, gain_cross, gain_ff, self_value, self_out, cross_query, cross_key, cross_value, cross_out, ff_in, ff_out = weights
    pair_count = lengths.shape[0]
    tokens = encoder_rows.shape[0]
    seg_ends = jnp.cumsum(lengths).astype(jnp.int32)
    starts = seg_ends - lengths
    places = jnp.arange(tokens, dtype=jnp.int32)[:, None]
    member = (places >= starts[None, :]) & (places < seg_ends[None, :])
    owner = lax.optimization_barrier(jnp.sum(member.astype(jnp.int32) * jnp.arange(pair_count, dtype=jnp.int32)[None, :], axis=1))
    normed = rms_norm(stream_in, gain_self)
    stream_one = stream_in + project(project(normed, self_value), self_out)
    normed = rms_norm(stream_one, gain_cross)
    queries = low(project(normed, cross_query)).reshape(pair_count, HEADS, HEAD_DIM)
    key_heads = low(project(encoder_rows, cross_key)).reshape(tokens, HEADS, HEAD_DIM)
    value_heads = low(project(encoder_rows, cross_value)).reshape(tokens, HEADS, HEAD_DIM)
    per_token = low_back(queries[owner])
    scores = lax.optimization_barrier(jnp.sum(per_token * key_heads, axis=-1))
    inside = member[:, :, None]
    highest = lax.optimization_barrier(jnp.max(jnp.where(inside, scores[:, None, :], -jnp.inf), axis=0))
    shifted = jnp.exp(scores - highest[owner])
    totals = lax.optimization_barrier(jnp.sum(jnp.where(inside, shifted[:, None, :], 0.0), axis=0))
    attend = shifted / totals[owner]
    weighted = low(attend[:, :, None] * value_heads).reshape(tokens, HEADS * HEAD_DIM)
    context = low_back(jnp.dot(member.T.astype(weighted.dtype), weighted, precision=lax.Precision.HIGHEST))
    stream_two = stream_one + project(context, cross_out)
    normed = rms_norm(stream_two, gain_ff)
    hidden = jax.nn.gelu(project(normed, ff_in))
    return stream_two + project(hidden, ff_out)

def reference(dec_in, encoded, seg_lengths, pair_slot, relevance, score_dir, gain_self, gain_cross, gain_ff, self_value, self_out, cross_query, cross_key, cross_value, cross_out, ff_in, ff_out):
    weights = tuple((weight.astype(jnp.float32) for weight in (gain_self, gain_cross, gain_ff, self_value, self_out, cross_query, cross_key, cross_value, cross_out, ff_in, ff_out)))
    direction = score_dir.astype(jnp.float32)
    group_total = MICRO * N_DP
    inputs_full = dec_in.astype(jnp.float32).reshape(group_total, PAIRS_MB, D)
    encoder_full = encoded.astype(jnp.float32).reshape(group_total, TOK_MB, D)
    lengths = seg_lengths.reshape(group_total, PAIRS_MB)
    inverse = jnp.argsort(pair_slot, axis=1).astype(jnp.int32)
    targets = jax.nn.softmax(relevance.reshape(MICRO, PAIRS_ALL // CAND, CAND), axis=-1)
    loss_weight = CAND * math.sqrt(D)

    def whole(weight_set, stream_in, encoder_rows):

        def one_group(group_item):
            return jax.checkpoint(group_layer)(weight_set, group_item[0], group_item[1], group_item[2])
        outputs = lax.map(one_group, (stream_in, encoder_rows, lengths))
        outputs = outputs.reshape(MICRO, PAIRS_ALL, D)
        scores = lax.optimization_barrier(jnp.sum(outputs * direction, axis=-1))
        by_slot = jnp.take_along_axis(scores, inverse, axis=1).reshape(MICRO, PAIRS_ALL // CAND, CAND)
        loss_value = -loss_weight * jnp.sum(targets * jax.nn.log_softmax(by_slot, axis=-1))
        return (loss_value, outputs)
    loss_value, pullback, outputs = jax.vjp(whole, weights, inputs_full, encoder_full, has_aux=True)
    grad_weights, grad_inputs, grad_encoder = pullback(jnp.ones((), jnp.float32))
    return (outputs.astype(jnp.float32), grad_inputs.reshape(MICRO, PAIRS_ALL, D).astype(jnp.float32), grad_encoder.reshape(MICRO, ENC_TOKENS, D).astype(jnp.bfloat16), grad_weights[0], grad_weights[1], grad_weights[2], grad_weights[3], grad_weights[4], grad_weights[5], grad_weights[6], grad_weights[7], grad_weights[8], grad_weights[9], grad_weights[10])
```

```python
import functools
import math

import jax
import jax.numpy as jnp
from jax import lax
from jax.experimental import pallas as pl
from jax.experimental.pallas import tpu as pltpu
from jax.sharding import PartitionSpec as P

MESH = pl.DeviceIdType.MESH
CAND = 16

def when(cond, fn):
    if isinstance(cond, bool):
        if cond: fn()
    else:
        pl.when(cond)(fn)

def gather_kernel(groups, rows_a, a_ref, b_ref, oa, ob, own, za, zb, ya, yb, xa, ca, ra, rb):
    lines = groups // 2
    d = lax.axis_index("dp")
    m = lax.axis_index("mp")
    o, i = d // 2, d % 2
    xm, cm = (m + 2) % 4, m + 1 - 2 * (m % 2)
    xcm = (cm + 2) % 4
    def dev(dd, mm):
        return (dd, mm)
    barrier = pltpu.get_barrier_semaphore()
    def hello(dd, mm):
        pl.semaphore_signal(barrier, inc=1, device_id=(dd, mm), device_id_type=MESH)
    hello(d + 1 - 2 * i, m); hello(d, xm); hello(d, cm)
    pl.when(o + 1 < lines)(lambda: hello(d + 2, m))
    pl.when(o > 0)(lambda: hello(d - 2, m))
    count = 3 + jnp.where(o + 1 < lines, 1, 0) + jnp.where(o > 0, 1, 0)
    pl.semaphore_wait(barrier, count)
    def put(src, dst, ssem, rsem, dd, mm):
        return pltpu.make_async_remote_copy(src_ref=src, dst_ref=dst, send_sem=ssem, recv_sem=rsem, device_id=(dd, mm), device_id_type=MESH)
    def a_at(mm, dd): return oa.at[mm, dd]
    def b_at(dd): return ob.at[dd]
    def send_a(dd, src, right, left, y, which_x, core):
        pass
    def right(dd, src_a, src_b):
        def go():
            put(src_a, a_at(m, dd), za.at[0, dd], ra.at[m, dd], d + 2, m).start()
            put(src_b, b_at(dd), zb.at[0, dd], rb.at[dd], d + 2, m).start()
        pl.when(o + 1 < lines)(go)
    def left(dd, src_a, src_b):
        def go():
            put(src_a, a_at(m, dd), za.at[1, dd], ra.at[m, dd], d - 2, m).start()
            put(src_b, b_at(dd), zb.at[1, dd], rb.at[dd], d - 2, m).start()
        pl.when(o > 0)(go)
    def yput(dd, src_a, src_b):
        put(src_a, a_at(m, dd), ya.at[dd], ra.at[m, dd], d + 1 - 2 * i, m).start()
        put(src_b, b_at(dd), yb.at[dd], rb.at[dd], d + 1 - 2 * i, m).start()
    def mates(dd, src_a):
        put(src_a, a_at(m, dd), xa.at[dd], ra.at[m, dd], d, xm).start()
        put(src_a, a_at(m, dd), ca.at[0, dd], ra.at[m, dd], d, cm).start()
    def got_a(mm, dd):
        put(a_at(mm, dd), a_at(mm, dd), xa.at[dd], ra.at[mm, dd], d, xm).wait_recv()
    def got_b(dd):
        put(b_at(dd), b_at(dd), yb.at[dd], rb.at[dd], d, xm).wait_recv()
    def from_x(dd):
        got_a(xm, dd)
        put(a_at(xm, dd), a_at(xm, dd), ca.at[1, dd], ra.at[xm, dd], d, cm).start()
    keep_a = pltpu.make_async_copy(a_ref, a_at(m, d), own.at[0])
    keep_b = pltpu.make_async_copy(b_ref, b_at(d), own.at[1])
    right(d, a_ref, b_ref); left(d, a_ref, b_ref); yput(d, a_ref, b_ref); mates(d, a_ref)
    keep_a.start(); keep_b.start()
    for k in range(1, lines):
        def west(k=k):
            dd = d - 2 * k
            got_a(m, dd); got_b(dd)
            right(dd, a_at(m, dd), b_at(dd)); yput(dd, a_at(m, dd), b_at(dd)); mates(dd, a_at(m, dd))
        pl.when(o - k >= 0)(west)
        def east(k=k):
            dd = d + 2 * k
            got_a(m, dd); got_b(dd)
            left(dd, a_at(m, dd), b_at(dd)); yput(dd, a_at(m, dd), b_at(dd)); mates(dd, a_at(m, dd))
        pl.when(o + k < lines)(east)
        if k == 1:
            from_x(d)
        else:
            pl.when(o - (k - 1) >= 0)(lambda k=k: from_x(d - 2 * (k - 1)))
            pl.when(o + (k - 1) < lines)(lambda k=k: from_x(d + 2 * (k - 1)))
    pl.when(o - (lines - 1) >= 0)(lambda: from_x(d - 2 * (lines - 1)))
    pl.when(o + (lines - 1) < lines)(lambda: from_x(d + 2 * (lines - 1)))
    dy = d + 1 - 2 * i
    def across(dd):
        got_a(m, dd); got_b(dd)
        mates(dd, a_at(m, dd))
    def order(fn, base):
        fn(base)
        for k in range(1, lines):
            pl.when(o - k >= 0)(lambda k=k: fn(base - 2 * k))
            pl.when(o + k < lines)(lambda k=k: fn(base + 2 * k))
    order(across, dy)
    order(from_x, dy)
    for dd in range(groups):
        got_a(cm, dd); got_a(xcm, dd)
    keep_a.wait(); keep_b.wait()
    def sent(src, sem):
        put(src, src, sem, ra.at[0, 0], d, xm).wait_send()
    for dd in range(groups):
        sent(a_at(m, dd), xa.at[dd]); sent(a_at(m, dd), ca.at[0, dd]); sent(a_at(m, dd), ca.at[1, dd])
    def line_sends(dd, oo):
        def r():
            sent(a_at(m, dd), za.at[0, dd]); sent(b_at(dd), zb.at[0, dd])
        def l():
            sent(a_at(m, dd), za.at[1, dd]); sent(b_at(dd), zb.at[1, dd])
        pl.when((oo <= o) & (o + 1 < lines))(r)
        pl.when((oo >= o) & (o > 0))(l)
        sent(a_at(m, dd), ya.at[dd]); sent(b_at(dd), yb.at[dd])
    for oo in range(lines):
        line_sends(oo * 2 + i, oo)

def gather(groups, a, b):
    ra, ca_ = a.shape
    out = (jax.ShapeDtypeStruct((4, groups) + a.shape, a.dtype), jax.ShapeDtypeStruct((groups,) + b.shape, b.dtype))
    S = pltpu.SemaphoreType.DMA
    return pl.pallas_call(functools.partial(gather_kernel, groups, ra), out_shape=out,
        in_specs=[pl.BlockSpec(memory_space=pl.ANY)] * 2, out_specs=[pl.BlockSpec(memory_space=pl.ANY)] * 2,
        scratch_shapes=[S((2,)), S((2, groups)), S((2, groups)), S((groups,)), S((groups,)), S((groups,)), S((2, groups)), S((4, groups)), S((groups,))],
        compiler_params=pltpu.CompilerParams(collective_id=0, has_side_effects=True), name="gather_weights")(a, b)

bf16, f32 = jnp.bfloat16, jnp.float32
D, HEAD, HEADS = 768, 64, 12
PER = HEADS // 4
WIN = 8
TILE = 256
eps = 1e-6
FAR = -1e30
VMEM = 60 << 20

def dot(a, b, ca=1, cb=0):
    return lax.dot_general(a, b, (((ca,), (cb,)), ((), ())), preferred_element_type=f32)

def exact(a, b):
    return lax.dot_general(a, b, (((1,), (0,)), ((), ())), preferred_element_type=f32, precision=lax.Precision.HIGHEST)

def rms(v):
    r = lax.rsqrt(jnp.mean(v * v, axis=-1, keepdims=True) + eps)
    return v * r, r

def head_of(shape, axis):
    return lax.broadcasted_iota(jnp.int32, shape, axis) // WIN

def expand(x):
    col = lax.broadcasted_iota(jnp.int32, x.shape, 1) // HEAD
    return jnp.concatenate([jnp.where(col == j, x, 0) for j in range(PER)], axis=0)

def collapse(x, rows):
    out = 0
    for j in range(PER):
        part = x[j * rows:(j + 1) * rows]
        col = lax.broadcasted_iota(jnp.int32, part.shape, 1) // HEAD
        out = out + jnp.where(col == j, part, 0)
    return out

def per_head(x, m, rows):
    col = lax.broadcasted_iota(jnp.int32, (rows, PER * HEAD), 1) // HEAD
    out = x[:, PER * m:PER * m + 1]
    out = jnp.where(col == 0, out, 0)
    for j in range(1, PER):
        out = jnp.where(col == j, x[:, PER * m + j:PER * m + j + 1], out)
    return out

def to_pairs(x):
    n = x.shape[0]
    wide = jnp.broadcast_to(x[:, None, :], (n, WIN, 128)).reshape(n * WIN, 128)
    lane = lax.broadcasted_iota(jnp.int32, wide.shape, 1)
    row = lax.broadcasted_iota(jnp.int32, wide.shape, 0)
    wide = jnp.where(lane % WIN == row % WIN, wide, 0.0)
    pick = (head_of((128, 128), 0) == lax.broadcasted_iota(jnp.int32, (128, 128), 1)).astype(f32)
    return exact(wide, pick)

def to_windows(x):
    pick = (lax.broadcasted_iota(jnp.int32, (128, 128), 0) == head_of((128, 128), 1)).astype(f32)
    wide = exact(x, pick)
    lane = lax.broadcasted_iota(jnp.int32, wide.shape, 1)
    row = lax.broadcasted_iota(jnp.int32, wide.shape, 0)
    wide = jnp.where(lane % WIN == row % WIN, wide, 0.0)
    return jnp.sum(wide.reshape(-1, WIN, 128), axis=1)

SV, SO, WQ, WK, WV, CO = 0, 192, 384, 576, 768, 960

def fill_windows(stage, m, rows, pairs):
    micro = stage.shape[0]
    n = micro * pairs
    for j in range(PER):
        h = PER * m + j
        stage[:, :, h * WIN:(h + 1) * WIN, :] = rows[j * n:(j + 1) * n].reshape(micro, pairs // WIN, WIN, D)

def front_kernel(micros, pairs, tiles, rank_ref, wlo, whi, x0_ref, a_hbm, enc_hbm, lo_ref, hi_ref,
                 x1_ref, v1_ref, q_ref, qk_ref, p_ref, c_ref, mx_ref, ctx_ref, lse_ref,
                 w_ref, enc, stage, s_scr, m_scr, l_scr, wsem, esem):
    wins = pairs // WIN
    span = tiles * TILE
    wcopy = pltpu.make_async_copy(a_hbm.at[:, :, 0:1024], w_ref, wsem)
    wcopy.start()
    base = rank_ref[0] * span
    def piece(u, t):
        return pltpu.make_async_copy(enc_hbm.at[u, pl.ds(pl.multiple_of(base + t * TILE, TILE), TILE), :],
                                     enc.at[u, pl.ds(t * TILE, TILE), :], esem.at[u, t])
    for u in range(micros):
        for t in range(tiles):
            piece(u, t).start()
    x0 = x0_ref[...].astype(f32)
    y1 = rms(x0)[0].astype(bf16)
    stage[:, :, HEADS * WIN:, :] = jnp.zeros((micros, wins, 128 - HEADS * WIN, D), f32)
    wcopy.wait()
    x1 = x0
    for m in range(4):
        v1 = dot(y1, w_ref[m, :, SV:SV + 192]).astype(bf16)
        v1_ref[m] = v1
        x1 = x1 + dot(v1, w_ref[m, :, SO:SO + 192], 1, 1)
    x1_ref[...] = x1
    y2 = rms(x1)[0].astype(bf16)
    for m in range(4):
        q = dot(y2, w_ref[m, :, WQ:WQ + 192]).astype(bf16)
        q_ref[m] = q
        fill_windows(stage, m, dot(expand(q), w_ref[m, :, WK:WK + 192], 1, 1), pairs)
    qk_ref[...] = stage[...].astype(bf16)
    stage[...] = jnp.zeros_like(stage)
    m_scr[...] = jnp.full(m_scr.shape, FAR, f32)
    l_scr[...] = jnp.zeros_like(l_scr)
    for u in range(micros):
        def first(t, _, u=u):
            piece(u, t).wait()
            rows = enc[u, pl.ds(pl.multiple_of(t * TILE, TILE), TILE), :]
            at = base + t * TILE + lax.broadcasted_iota(jnp.int32, (TILE, 128), 0)
            def block(w, _):
                s = dot(rows, qk_ref[u, w], 1, 1)
                s = jnp.where((at >= lo_ref[u, w]) & (at < hi_ref[u, w]), s, FAR)
                s_scr[t + w - wlo[u, 0]] = s
                m_scr[u, w] = jnp.maximum(m_scr[u, w], jnp.max(s, axis=0, keepdims=True))
                return 0
            return lax.fori_loop(wlo[u, t], whi[u, t] + 1, block, 0)
        lax.fori_loop(0, tiles, first, 0)
        def second(t, _, u=u):
            rows = enc[u, pl.ds(pl.multiple_of(t * TILE, TILE), TILE), :]
            def block(w, _):
                k = t + w - wlo[u, 0]
                s = s_scr[k]
                p = jnp.where(s > FAR, jnp.exp(s - m_scr[u, w]), 0.0)
                l_scr[u, w] = l_scr[u, w] + jnp.sum(p, axis=0, keepdims=True)
                low = p.astype(bf16)
                p_ref[u, k] = low
                stage[u, w] = stage[u, w] + dot(low, rows, 0, 0)
                return 0
            return lax.fori_loop(wlo[u, t], whi[u, t] + 1, block, 0)
        lax.fori_loop(0, tiles, second, 0)
    n = micros * pairs
    mx = to_pairs(m_scr[...].reshape(micros * wins, 128))
    lx = to_pairs(l_scr[...].reshape(micros * wins, 128))
    some = lx > 0.0
    inv = jnp.where(some, 1.0 / jnp.where(some, lx, 1.0), 0.0)
    mx_ref[...] = mx
    lse_ref[...] = jnp.where(some, mx + jnp.log(jnp.where(some, lx, 1.0)), FAR)
    for h in range(HEADS):
        rows = stage[:, :, h * WIN:(h + 1) * WIN, :].reshape(n, D) * inv[:, h:h + 1]
        c_ref[h] = rows.astype(bf16)
    for m in range(4):
        rows = c_ref[PER * m:PER * (m + 1)].reshape(PER * n, D)
        ctx_ref[m] = collapse(dot(rows, w_ref[m, :, WV:WV + 192]), n).astype(bf16)

def front(rank, wlo, whi, x0, a_full, encoded, lo, hi):
    micros, pairs = encoded.shape[0], x0.shape[0] // encoded.shape[0]
    tiles = wlo.shape[1]
    wins = pairs // WIN
    n = micros * pairs
    steps = tiles + wins - 1
    sd = jax.ShapeDtypeStruct
    any_, vm, sm = (pl.BlockSpec(memory_space=s) for s in (pl.ANY, pltpu.VMEM, pltpu.SMEM))
    return pl.pallas_call(
        functools.partial(front_kernel, micros, pairs, tiles),
        out_shape=(sd((n, D), f32), sd((4, n, 192), bf16), sd((4, n, 192), bf16), sd((micros, wins, 128, D), bf16),
                   sd((micros, steps, TILE, 128), bf16), sd((HEADS, n, D), bf16), sd((n, 128), f32), sd((4, n, 192), bf16), sd((n, 128), f32)),
        in_specs=[sm, sm, sm, vm, any_, any_, vm, vm],
        out_specs=[vm] * 9,
        scratch_shapes=[pltpu.VMEM((4, D, 1024), bf16), pltpu.VMEM((micros, tiles * TILE, D), bf16),
                        pltpu.VMEM((micros, wins, 128, D), f32), pltpu.VMEM((steps, TILE, 128), f32),
                        pltpu.VMEM((micros, wins, 1, 128), f32), pltpu.VMEM((micros, wins, 1, 128), f32),
                        pltpu.SemaphoreType.DMA, pltpu.SemaphoreType.DMA((micros, tiles))],
        compiler_params=pltpu.CompilerParams(vmem_limit_bytes=VMEM),
        name="attention_forward",
    )(rank, wlo, whi, x0, a_full, encoded, lo, hi)

def back_kernel(micros, pairs, tiles, rank_ref, wlo, whi, enc_ref, a_hbm, qk_ref, p_ref, c_ref, mx_ref, lse_loc, lse_ref, delta_ref, dctx_ref, q_ref,
                de_ref, dq_ref, gkv_ref, w_ref, stage, qu, alpha, delta, acc, wsem):
    wins = pairs // WIN
    n = micros * pairs
    g = pl.program_id(0)
    u, t = g // tiles, g % tiles
    wcopy = pltpu.make_async_copy(a_hbm.at[:, :, 512:1024], w_ref, wsem)
    @pl.when(g == 0)
    def _():
        wcopy.start()
        lse = lse_ref[...]
        alpha[...] = to_windows(jnp.exp(jnp.minimum(mx_ref[...] - lse, 1.0))).reshape(alpha.shape)
        delta[...] = to_windows(delta_ref[...]).reshape(delta.shape)
        qu[:, :, 0:128, :] = qk_ref[...]
        stage[:, :, HEADS * WIN:, :] = jnp.zeros((micros, wins, 128 - HEADS * WIN, D), f32)
        share = jnp.exp(jnp.minimum(lse_loc[...] - lse, 1.0))
        wcopy.wait()
        for m in range(4):
            dctx = expand(dctx_ref[m])
            fill_windows(stage, m, dot(dctx, w_ref[m, :, 256:448], 1, 1), pairs)
            scaled = jnp.concatenate([dctx[j * n:(j + 1) * n] * share[:, PER * m + j:PER * m + j + 1].astype(bf16) for j in range(PER)], axis=0)
            gkv_ref[m, :, 192:384] = dot(c_ref[PER * m:PER * (m + 1)].reshape(PER * n, D), scaled, 0, 0).astype(bf16)
        qu[:, :, 128:256, :] = stage[...].astype(bf16)
        stage[...] = jnp.zeros_like(stage)
    rows = enc_ref[0]
    first = wlo[u, t]
    def block(w):
        da = dot(rows, qu[u, w, 128:256, :], 1, 1)
        a = p_ref[u, t + w - wlo[u, 0]].astype(f32) * alpha[u, w]
        ds = a * (da - delta[u, w])
        both = jnp.concatenate([ds.astype(bf16), a.astype(bf16)], axis=1)
        stage[u, w] = stage[u, w] + dot(both[:, 0:128], rows, 0, 0)
        return dot(both, qu[u, w])
    acc[...] = block(first)
    def more(w, _):
        acc[...] = acc[...] + block(w)
        return 0
    lax.fori_loop(first + 1, whi[u, t] + 1, more, 0)
    de_ref[0] = acc[...].astype(bf16)
    @pl.when(g == micros * tiles - 1)
    def _():
        for m in range(4):
            e = jnp.concatenate([stage[:, :, h * WIN:(h + 1) * WIN, :].reshape(n, D).astype(bf16) for h in range(PER * m, PER * (m + 1))], axis=0)
            dq_ref[m] = collapse(dot(e, w_ref[m, :, 64:256]), n).astype(bf16)
            gkv_ref[m, :, 0:192] = dot(e, expand(q_ref[m]), 0, 0).astype(bf16)

def back(rank, wlo, whi, encoded, a_full, qk, p, c, mx, lse_loc, lse, delta, dctx, q):
    micros, n = encoded.shape[0], mx.shape[0]
    pairs = n // micros
    tiles = wlo.shape[1]
    wins = pairs // WIN
    sd = jax.ShapeDtypeStruct
    def whole(x):
        return pl.BlockSpec(x.shape, lambda g, *_: (0,) * x.ndim)
    rest = (qk, p, c, mx, lse_loc, lse, delta, dctx, q)
    return pl.pallas_call(
        functools.partial(back_kernel, micros, pairs, tiles),
        out_shape=(sd((micros, tiles * TILE, D), bf16), sd((4, n, 192), bf16), sd((4, D, 384), bf16)),
        grid_spec=pltpu.PrefetchScalarGridSpec(
            num_scalar_prefetch=3, grid=(micros * tiles,),
            in_specs=[pl.BlockSpec((1, TILE, D), lambda g, r, lo, hi: (g // tiles, r[0] * tiles + g % tiles, 0)),
                      pl.BlockSpec(memory_space=pl.ANY)] + [whole(x) for x in rest],
            out_specs=[pl.BlockSpec((1, TILE, D), lambda g, r, lo, hi: (g // tiles, g % tiles, 0)),
                       pl.BlockSpec((4, n, 192), lambda g, *_: (0, 0, 0)), pl.BlockSpec((4, D, 384), lambda g, *_: (0, 0, 0))],
            scratch_shapes=[pltpu.VMEM((4, D, 512), bf16), pltpu.VMEM((micros, wins, 128, D), f32), pltpu.VMEM((micros, wins, 256, D), bf16),
                            pltpu.VMEM((micros, wins, 1, 128), f32), pltpu.VMEM((micros, wins, 1, 128), f32), pltpu.VMEM((TILE, D), f32),
                            pltpu.SemaphoreType.DMA]),
        compiler_params=pltpu.CompilerParams(vmem_limit_bytes=VMEM, dimension_semantics=("arbitrary",)),
        name="attention_backward",
    )(rank, wlo, whi, encoded, a_full, *rest)

def plan(seg_lengths, rank, tokens):
    micros, pairs = seg_lengths.shape
    ends = jnp.cumsum(seg_lengths, axis=1)
    starts = ends - seg_lengths
    span = tokens // 4
    tiles = span // TILE
    firsts = rank * span + TILE * jnp.arange(tiles, dtype=jnp.int32)
    def window(at):
        return jnp.sum((ends[:, None, :] <= at[None, :, None]).astype(jnp.int32), axis=-1) // WIN
    wlo, whi = window(firsts), window(firsts + (TILE - 1))
    def lanes(x):
        x = jnp.broadcast_to(x.reshape(micros, pairs // WIN, 1, 1, WIN), (micros, pairs // WIN, 1, HEADS, WIN))
        return jnp.pad(x.reshape(micros, pairs // WIN, 1, HEADS * WIN), ((0, 0), (0, 0), (0, 0), (0, 128 - HEADS * WIN)))
    return wlo, whi, lanes(starts), lanes(ends)

def put(src, dst, ssem, rsem, where):
    return pltpu.make_async_remote_copy(src_ref=src, dst_ref=dst, send_sem=ssem, recv_sem=rsem, device_id=where, device_id_type=MESH)

def flips(m):
    return (m + 2) % 4, m + 1 - 2 * (m % 2)

def gelu(u):
    c = math.sqrt(2.0 / math.pi)
    t = jnp.tanh(c * (u + 0.044715 * u * u * u))
    return 0.5 * u * (1.0 + t), 0.5 * (1.0 + t) + 0.5 * u * (1.0 - t * t) * c * (1.0 + 3 * 0.044715 * u * u)

def norm_back(y, r, pushed):
    return r * (pushed - y * jnp.mean(pushed * y, axis=-1, keepdims=True))

def merge(ca, la, cb, lb):
    top = jnp.maximum(la, lb)
    ea, eb = jnp.exp(la - top), jnp.exp(lb - top)
    total = ea + eb
    wa, wb = ea / total, eb / total
    n = la.shape[0]
    return [ca[m].astype(f32) * per_head(wa, m, n) + cb[m].astype(f32) * per_head(wb, m, n) for m in range(4)], top + jnp.log(total)

def middle_kernel(groups, weight, ctxl_ref, lsel_ref, x1_ref, a_hbm, b_hbm, dir_ref, keyc, slotc, keyr, slotr, rel_ref,
                  ctx_ref, lse_ref, dctx_ref, delta_ref, x3_ref, dx2_ref, y3_ref, du_ref, p3_ref, hs_ref,
                  co, ffi, ffo, cbuf, lbuf, cmid, lmid, msgs, hsum, xbuf, xmid, nbuf, nmid,
                  lsem, csem, crec, msem, mrec, hsem, hrec, xsem, xrec, nsem, nrec):
    n = x1_ref.shape[0]
    total = 4 * groups
    d, m = lax.axis_index("dp"), lax.axis_index("mp")
    me = d * 4 + m
    xm, cm = flips(m)
    loads = [pltpu.make_async_copy(a_hbm.at[:, :, 896:1152], co, lsem.at[0]),
             pltpu.make_async_copy(b_hbm.at[:, 0:768], ffi, lsem.at[1]),
             pltpu.make_async_copy(b_hbm.at[:, 768:1536], ffo, lsem.at[2])]
    for load in loads:
        load.start()
    barrier = pltpu.get_barrier_semaphore()
    def hello(j, _):
        to = (me + j) % total
        pl.semaphore_signal(barrier, inc=1, device_id=(to // 4, to % 4), device_id_type=MESH)
        return 0
    lax.fori_loop(1, total, hello, 0)
    pl.semaphore_wait(barrier, total - 1)
    hop = [put(ctxl_ref, cbuf.at[0], csem.at[0], crec.at[0], (d, cm)), put(lsel_ref, lbuf.at[0], csem.at[1], crec.at[1], (d, cm))]
    for c in hop:
        c.start()
    for c in hop:
        c.wait()
    both, lse = merge(ctxl_ref, lsel_ref[...], cbuf.at[0], lbuf[0])
    for k in range(4):
        cmid[k] = both[k].astype(bf16)
    lmid[...] = lse
    hop = [put(cmid, cbuf.at[1], csem.at[2], crec.at[2], (d, xm)), put(lmid, lbuf.at[1], csem.at[3], crec.at[3], (d, xm))]
    for c in hop:
        c.start()
    for load in loads:
        load.wait()
    direction = dir_ref[...]
    fd = dot(jnp.broadcast_to(direction, (8, D)).astype(bf16), ffo[...])[0:1]
    for c in hop:
        c.wait()
    both, lse = merge(cmid, lmid[...], cbuf.at[1], lbuf[1])
    lse_ref[...] = lse
    x2 = x1_ref[...]
    for k in range(4):
        low = both[k].astype(bf16)
        ctx_ref[k] = low
        x2 = x2 + dot(low, co[k, :, 64:256], 1, 1)
    y3, r3 = rms(x2)
    y3b = y3.astype(bf16)
    y3_ref[...] = y3b
    act, slope = gelu(dot(y3b, ffi[...]))
    hid = act.astype(bf16)
    hidf = hid.astype(f32)
    score = jnp.sum(hidf * fd, axis=1, keepdims=True) + jnp.where(m == 0, jnp.sum(x2 * direction, axis=1, keepdims=True), 0.0)
    eye = lax.broadcasted_iota(jnp.int32, (n, n), 0) == lax.broadcasted_iota(jnp.int32, (n, n), 1)
    row = jnp.sum(jnp.where(eye, score, 0.0), axis=0, keepdims=True)
    line = lax.broadcasted_iota(jnp.int32, (8, n), 0)
    msgs[me] = jnp.where(line == 0, row, jnp.where(line == 1, rel_ref[...], 0.0))
    def tell(j, _):
        to = (me + j) % total
        put(msgs.at[me], msgs.at[me], msem.at[j], mrec.at[me], (to // 4, to % 4)).start()
        return 0
    lax.fori_loop(1, total, tell, 0)
    x3p = dot(hid, ffo[...], 1, 1)
    xmid[0] = x3p.astype(bf16)
    xhop = put(xmid.at[0], xbuf.at[0], xsem.at[0], xrec.at[0], (d, cm))
    xhop.start()
    def hear(j, _):
        to = (me + j) % total
        put(msgs.at[to], msgs.at[to], msem.at[j], mrec.at[to], (to // 4, to % 4)).wait_recv()
        put(msgs.at[me], msgs.at[me], msem.at[j], mrec.at[me], (to // 4, to % 4)).wait_send()
        return 0
    lax.fori_loop(1, total, hear, 0)
    kc, sc = keyc[...], slotc[...]
    lane = lax.broadcasted_iota(jnp.int32, (1, n), 1)
    half = n // 2
    def rows_of(g):
        s = (msgs[4 * g] + msgs[4 * g + 1] + msgs[4 * g + 2] + msgs[4 * g + 3])[0:1]
        rel = msgs[4 * g][1:2]
        slot = (lane // half) * (groups * half) + g * half + lane % half
        return s, rel, keyr[pl.ds(g, 1), :] == kc, slotr[pl.ds(g, 1), :] == sc, slot // 16 == kc, slot == sc
    def tops(g, carry):
        a, b, own, rown = carry
        s, rel, same, mine, rsame, rmine = rows_of(g)
        return (jnp.maximum(a, jnp.where(same, s, FAR)), jnp.maximum(b, jnp.where(rsame, rel, FAR)),
                own + jnp.where(mine, s, 0.0), rown + jnp.where(rmine, rel, 0.0))
    z = jnp.zeros((n, n), f32)
    far = jnp.full((n, n), FAR, f32)
    a, b, own, rown = lax.fori_loop(0, groups, tops, (far, far, z, z), unroll=groups <= 8)
    a, b = jnp.max(a, axis=1, keepdims=True), jnp.max(b, axis=1, keepdims=True)
    own, rown = jnp.sum(own, axis=1, keepdims=True), jnp.sum(rown, axis=1, keepdims=True)
    def sums(g, carry):
        s, rel, same, _, rsame, _ = rows_of(g)
        return (carry[0] + jnp.where(same, jnp.exp(s - a), 0.0), carry[1] + jnp.where(rsame, jnp.exp(rel - b), 0.0))
    sa, sb = lax.fori_loop(0, groups, sums, (z, z), unroll=groups <= 8)
    dscore = weight * (jnp.exp(own - a) / jnp.sum(sa, axis=1, keepdims=True) - jnp.exp(rown - b) / jnp.sum(sb, axis=1, keepdims=True))
    du = (slope * dscore * fd).astype(bf16)
    du_ref[...] = du
    nmid[0] = dot(du, ffi[...], 1, 1).astype(bf16)
    nhop = put(nmid.at[0], nbuf.at[0], nsem.at[0], nrec.at[0], (d, cm))
    nhop.start()
    hsum[d] = jnp.broadcast_to(jnp.sum(hidf * dscore, axis=0, keepdims=True), (8, D))
    def spread(j, _):
        to = (d + j) % groups
        put(hsum.at[d], hsum.at[d], hsem.at[j], hrec.at[d], (to, m)).start()
        return 0
    lax.fori_loop(1, groups, spread, 0)
    nhop.wait()
    part = nmid[0].astype(f32) + nbuf[0].astype(f32)
    nmid[1] = part.astype(bf16)
    nhop = put(nmid.at[1], nbuf.at[1], nsem.at[1], nrec.at[1], (d, xm))
    nhop.start()
    xhop.wait()
    xpart = x3p + xbuf[0].astype(f32)
    xmid[1] = xpart.astype(bf16)
    xhop = put(xmid.at[1], xbuf.at[1], xsem.at[1], xrec.at[1], (d, xm))
    xhop.start()
    nhop.wait()
    dn3 = part + nbuf[1].astype(f32)
    p3_ref[...] = (dn3 * y3).astype(bf16)
    dx2 = dscore * direction + norm_back(y3, r3, dn3)
    dx2_ref[...] = dx2
    gc = dx2.astype(bf16)
    delta = jnp.zeros((n, 128), f32)
    for k in range(4):
        dctx = dot(gc, co[k, :, 64:256]).astype(bf16)
        dctx_ref[k] = dctx
        pick = (lax.broadcasted_iota(jnp.int32, (192, 128), 0) // HEAD + PER * k == lax.broadcasted_iota(jnp.int32, (192, 128), 1)).astype(f32)
        delta = delta + exact(dctx.astype(f32) * both[k], pick)
    delta_ref[...] = delta
    xhop.wait()
    x3_ref[...] = x2 + xpart + xbuf[1].astype(f32)
    def gathered(j, acc):
        to = (d + j) % groups
        put(hsum.at[to], hsum.at[to], hsem.at[j], hrec.at[to], (to, m)).wait_recv()
        put(hsum.at[d], hsum.at[d], hsem.at[j], hrec.at[d], (to, m)).wait_send()
        return acc + hsum[to]
    hs_ref[...] = lax.fori_loop(1, groups, gathered, hsum[d])

def middle(groups, weight, ctxl, lsel, x1, a_full, b_full, direction, keyc, slotc, keyr, slotr, rel):
    n = x1.shape[0]
    sd = jax.ShapeDtypeStruct
    any_, vm = (pl.BlockSpec(memory_space=s) for s in (pl.ANY, pltpu.VMEM))
    S, V = pltpu.SemaphoreType.DMA, pltpu.VMEM
    return pl.pallas_call(
        functools.partial(middle_kernel, groups, weight),
        out_shape=(sd((4, n, 192), bf16), sd((n, 128), f32), sd((4, n, 192), bf16), sd((n, 128), f32), sd((n, D), f32), sd((n, D), f32),
                   sd((n, D), bf16), sd((n, D), bf16), sd((n, D), bf16), sd((8, D), f32)),
        in_specs=[vm, vm, vm, any_, any_] + [vm] * 6, out_specs=[vm] * 10,
        scratch_shapes=[V((4, D, 256), bf16), V((D, D), bf16), V((D, D), bf16), V((2, 4, n, 192), bf16), V((2, n, 128), f32), V((4, n, 192), bf16), V((n, 128), f32),
                        V((4 * groups, 8, n), f32), V((groups, 8, D), f32), V((2, n, D), bf16), V((2, n, D), bf16), V((2, n, D), bf16), V((2, n, D), bf16),
                        S((3,)), S((4,)), S((4,)), S((4 * groups,)), S((4 * groups,)), S((groups,)), S((groups,)), S((2,)), S((2,)), S((2,)), S((2,))],
        compiler_params=pltpu.CompilerParams(collective_id=1, has_side_effects=True, vmem_limit_bytes=VMEM),
        name="feed_forward",
    )(ctxl, lsel, x1, a_full, b_full, direction, keyc, slotc, keyr, slotr, rel)

def tail_kernel(groups, dqp_ref, gkv_ref, x0_ref, x1_ref, dx2_ref, v1_ref, ctx_ref, y3_ref, du_ref, p3_ref, a_hbm,
                dx0_ref, out0, out1,
                w, dqm, dqb, dqs, dvs, kvb, kvx, kvs, r0, r1, yb0, yb1, ys0, ys1, zl0, zl1, zr0, zr1,
                wsem, qsem, qrec, ksem, krec, ysem, yrec, zsem, zrec):
    n = x0_ref.shape[0]
    lines = groups // 2
    rows = D // groups
    d, m = lax.axis_index("dp"), lax.axis_index("mp")
    o, i = d // 2, d % 2
    dy = d + 1 - 2 * i
    xm, cm = flips(m)
    xcm = (cm + 2) % 4
    load = pltpu.make_async_copy(a_hbm.at[:, :, 0:640], w, wsem)
    load.start()
    barrier = pltpu.get_barrier_semaphore()
    def hello(dd, mm):
        pl.semaphore_signal(barrier, inc=1, device_id=(dd, mm), device_id_type=MESH)
    hello(dy, m); hello(d, xm); hello(d, cm)
    pl.when(o + 1 < lines)(lambda: hello(d + 2, m))
    pl.when(o > 0)(lambda: hello(d - 2, m))
    pl.semaphore_wait(barrier, 3 + jnp.where(o + 1 < lines, 1, 0) + jnp.where(o > 0, 1, 0))
    qhop = put(dqp_ref, dqb.at[0], qsem.at[0], qrec.at[0], (d, cm))
    qhop.start()
    khops = [put(gkv_ref.at[cm], kvb.at[0], ksem.at[0], krec.at[0], (d, cm)), put(gkv_ref.at[xcm], kvb.at[1], ksem.at[1], krec.at[1], (d, cm))]
    for c in khops:
        c.start()
    def keep(ref, value):
        for g in range(groups):
            ref[g] = value[g * rows:(g + 1) * rows].astype(bf16)
    ones = jnp.ones((n, 64), bf16)
    lane = lax.broadcasted_iota(jnp.int32, (n, 64), 1)
    y3 = y3_ref[...]
    gc = dx2_ref[...].astype(bf16)
    keep(r0, jnp.concatenate([dot(y3, du_ref[...], 0, 0), dot(gc, ctx_ref[m], 0, 0), dot(p3_ref[...], ones, 0, 0)], axis=1))
    def across(k, r, yb):
        return [put(r.at[2 * oo + 1 - i], yb.at[oo], ysem.at[k, oo], yrec.at[k, oo], (dy, m)) for oo in range(lines)]
    y0 = across(0, r0, yb0)
    for c in y0:
        c.start()
    qhop.wait()
    for k in range(4):
        dqm[k] = (dqp_ref[k].astype(f32) + dqb[0, k].astype(f32)).astype(bf16)
    qhop = put(dqm, dqb.at[1], qsem.at[1], qrec.at[1], (d, xm))
    qhop.start()
    for c in khops:
        c.wait()
    kvs[...] = (gkv_ref[xm].astype(f32) + kvb[1].astype(f32)).astype(bf16)
    khop = put(kvs, kvx, ksem.at[2], krec.at[2], (d, xm))
    khop.start()
    load.wait()
    x1 = x1_ref[...]
    y1, g1 = rms(x0_ref[...].astype(f32))
    y2, g2 = rms(x1)
    qhop.wait()
    dn2 = 0
    for k in range(4):
        dq = (dqm[k].astype(f32) + dqb[1, k].astype(f32)).astype(bf16)
        dqs[k] = dq
        dn2 = dn2 + dot(dq, w[k, :, WQ:WQ + 192], 1, 1)
    dx1 = dx2_ref[...] + norm_back(y2, g2, dn2)
    gs = dx1.astype(bf16)
    dn1 = 0
    for k in range(4):
        dv = dot(gs, w[k, :, SO:SO + 192]).astype(bf16)
        dvs[k] = dv
        dn1 = dn1 + dot(dv, w[k, :, SV:SV + 192], 1, 1)
    dx0_ref[...] = dx1 + norm_back(y1, g1, dn1)
    small = [dot(y1.astype(bf16), dvs[m], 0, 0), dot(gs, v1_ref[m], 0, 0), dot(y2.astype(bf16), dqs[m], 0, 0)]
    gains = (dot((dn1 * y1).astype(bf16), jnp.where(lane < 32, ones, 0), 0, 0) + dot((dn2 * y2).astype(bf16), jnp.where(lane < 32, 0, ones), 0, 0))
    khop.wait()
    kv = gkv_ref[m].astype(f32) + kvb[0].astype(f32) + kvx[...].astype(f32)
    keep(r1, jnp.concatenate(small + [kv, gains], axis=1))
    y1c = across(1, r1, yb1)
    for c in y1c:
        c.start()
    def line(k, copies, r, yb, ys, zl, zr):
        for oo in range(lines):
            copies[oo].wait()
            ys[oo] = (r[2 * oo + i].astype(f32) + yb[oo].astype(f32)).astype(bf16)
        def right(t):
            return put(ys.at[t], zl.at[t], zsem.at[k, t], zrec.at[k, 0, t], (d + 2, m))
        def left(t):
            return put(ys.at[t], zr.at[t], zsem.at[k, t], zrec.at[k, 1, t], (d - 2, m))
        def from_left(t):
            put(ys.at[t], zl.at[t], zsem.at[k, t], zrec.at[k, 0, t], (d - 2, m)).wait_recv()
        def from_right(t):
            put(ys.at[t], zr.at[t], zsem.at[k, t], zrec.at[k, 1, t], (d + 2, m)).wait_recv()
        def add(t, z):
            ys[t] = (ys[t].astype(f32) + z[t].astype(f32)).astype(bf16)
        for j in range(lines - 1):
            t = lines - 1 - j
            def go_right(t=t):
                @pl.when(o > 0)
                def _():
                    from_left(t)
                    add(t, zl)
                right(t).start()
            pl.when(o < t)(go_right)
            s = j
            def go_left(s=s):
                @pl.when(o < lines - 1)
                def _():
                    from_right(s)
                    add(s, zr)
                left(s).start()
            pl.when(o > s)(go_left)
        def finish(out):
            out[...] = ys[o].astype(f32)
            @pl.when(o > 0)
            def _():
                from_left(o)
                out[...] = out[...] + zl[o].astype(f32)
            @pl.when(o < lines - 1)
            def _():
                from_right(o)
                out[...] = out[...] + zr[o].astype(f32)
            for t in range(lines):
                pl.when(o < t)(lambda t=t: right(t).wait_send())
                pl.when(o > t)(lambda t=t: left(t).wait_send())
        return finish
    f0 = line(0, y0, r0, yb0, ys0, zl0, zr0)
    f1 = line(1, y1c, r1, yb1, ys1, zl1, zr1)
    f0(out0)
    f1(out1)

def tail(groups, dqp, gkv, x0, x1, dx2, v1, ctx, y3, du, p3, a_full):
    n = x0.shape[0]
    rows, lines = D // groups, groups // 2
    sd = jax.ShapeDtypeStruct
    any_, vm = (pl.BlockSpec(memory_space=s) for s in (pl.ANY, pltpu.VMEM))
    S, V = pltpu.SemaphoreType.DMA, pltpu.VMEM
    blocks = lambda k: V((k, rows, 1024), bf16)
    return pl.pallas_call(
        functools.partial(tail_kernel, groups),
        out_shape=(sd((n, D), f32), sd((rows, 1024), f32), sd((rows, 1024), f32)),
        in_specs=[vm] * 10 + [any_], out_specs=[vm] * 3,
        scratch_shapes=[V((4, D, 640), bf16), V((4, n, 192), bf16), V((2, 4, n, 192), bf16), V((4, n, 192), bf16), V((4, n, 192), bf16),
                        V((2, D, 384), bf16), V((D, 384), bf16), V((D, 384), bf16), blocks(groups), blocks(groups)] + [blocks(lines)] * 8 +
                       [S, S((2,)), S((2,)), S((3,)), S((3,)), S((2, lines)), S((2, lines)), S((2, lines)), S((2, 2, lines))],
        compiler_params=pltpu.CompilerParams(collective_id=2, has_side_effects=True, vmem_limit_bytes=VMEM),
        name="gradient_sums",
    )(dqp, gkv, x0, x1, dx2, v1, ctx, y3, du, p3, a_full)

def shards(dec_in, encoded, seg_lengths, pair_slot, relevance, score_dir, gain_self, gain_cross, gain_ff,
           self_value, self_out, cross_query, cross_key, cross_value, cross_out, ff_in, ff_out):
    micros, pairs = dec_in.shape[0], dec_in.shape[1]
    n = micros * pairs
    groups = lax.axis_size("dp")
    d, m = lax.axis_index("dp"), lax.axis_index("mp")
    gains = [g.astype(f32)[:, None] for g in (gain_self, gain_cross, gain_ff)]
    def scaled(g, weight):
        return (g * weight.astype(f32)).astype(bf16)
    a_own = jnp.concatenate([scaled(gains[0], self_value), self_out.T, scaled(gains[1], cross_query), cross_key, cross_value, cross_out.T], axis=1)
    b_own = jnp.concatenate([scaled(gains[2], ff_in), ff_out.T], axis=1)
    a_full, b_full = gather(groups, a_own, b_own)
    a_full, b_full = a_full.reshape(4, D, 1152), b_full.reshape(D, 1536)
    rank = jnp.reshape(m, (1,)).astype(jnp.int32)
    wlo, whi, lo, hi = plan(seg_lengths[:, 0], m, encoded.shape[1])
    x0 = dec_in.reshape(n, D)
    x1, v1, q, qk, p, c, mx, ctxl, lsel = front(rank, wlo, whi, x0, a_full, encoded, lo, hi)
    everyone = groups * pairs
    slots = pair_slot + everyone * jnp.arange(micros, dtype=jnp.int32)[:, None]
    slotr = slots.reshape(micros, groups, pairs).transpose(1, 0, 2).reshape(groups, n)
    slotc = lax.dynamic_slice_in_dim(slotr, d, 1, 0).reshape(n, 1)
    direction = score_dir.astype(f32)
    ctx, lse, dctx, delta, x3, dx2, y3, du, p3, hs = middle(
        groups, CAND * math.sqrt(D), ctxl, lsel, x1, a_full, b_full, direction.reshape(1, D),
        slotc // CAND, slotc, slotr // CAND, slotr, relevance.reshape(1, n))
    d_encoded, dqp, gkv = back(rank, wlo, whi, encoded, a_full, qk, p, c, mx, lsel, lse, delta, dctx, q)
    dx0, sum0, sum1 = tail(groups, dqp, gkv, x0, x1, dx2, v1, ctx, y3, du, p3, a_full)
    here = lax.dynamic_slice_in_dim(direction, d * (D // groups), D // groups)
    return (
        x3.reshape(micros, pairs, D),
        dx0.reshape(micros, pairs, D),
        d_encoded,
        sum1[:, 960] / gains[0][:, 0],
        sum1[:, 992] / gains[1][:, 0],
        sum0[:, 960] / gains[2][:, 0],
        sum1[:, 0:192] * gains[0],
        sum1[:, 192:384].T,
        sum1[:, 384:576] * gains[1],
        sum1[:, 576:768],
        sum1[:, 768:960],
        sum0[:, 768:960].T,
        sum0[:, 0:768] * gains[2],
        hs[0][:, None] * here[None, :],
    )


def solution(mesh):
    in_specs = (
        P(None, "dp", None),
        P(None, "dp", None),
        P(None, "dp", None),
        P(),
        P(None, "dp"),
        P(),
        P("dp"),
        P("dp"),
        P("dp"),
        P("dp", "mp"),
        P("mp", "dp"),
        P("dp", "mp"),
        P("dp", "mp"),
        P("dp", "mp"),
        P("mp", "dp"),
        P("dp", "mp"),
        P("mp", "dp"),
    )
    out_specs = (
        P(None, "dp", None),
        P(None, "dp", None),
        P(None, ("dp", "mp"), None),
        P("dp"),
        P("dp"),
        P("dp"),
        P("dp", "mp"),
        P("mp", "dp"),
        P("dp", "mp"),
        P("dp", "mp"),
        P("dp", "mp"),
        P("mp", "dp"),
        P("dp", "mp"),
        P("mp", "dp"),
    )
    return jax.shard_map(shards, mesh=mesh, in_specs=in_specs, out_specs=out_specs, check_vma=False)
```

```python
import functools
import math

import jax
import jax.numpy as jnp
from jax import lax
from jax.experimental import pallas as pl
from jax.experimental.pallas import tpu as pltpu
from jax.sharding import PartitionSpec as P

MESH = pl.DeviceIdType.MESH
bf16, f32 = jnp.bfloat16, jnp.float32
CAND = 16
D, HEAD, HEADS = 768, 64, 12
PER = HEADS // 4
WIDE = PER * HEAD
WIN = 8
COLS = HEADS * WIN
TILE = 256
eps = 1e-6
FAR = -1e30
VMEM = 63 << 20
UNROLL = 2
OUTS = 2


def dot(a, b, ca=1, cb=0):
    return lax.dot_general(a, b, (((ca,), (cb,)), ((), ())), preferred_element_type=f32)


def exact(a, b):
    return lax.dot_general(a, b, (((1,), (0,)), ((), ())), preferred_element_type=f32, precision=lax.Precision.HIGHEST)


def iota(shape, axis):
    return lax.broadcasted_iota(jnp.int32, shape, axis)


def to_column(row):
    k = row.shape[1]
    return jnp.sum(jnp.where(iota((k, k), 0) == iota((k, k), 1), row, 0.0), axis=1, keepdims=True)


def to_row(column):
    k = column.shape[0]
    return jnp.sum(jnp.where(iota((k, k), 0) == iota((k, k), 1), column, 0.0), axis=0, keepdims=True)


def fold_row(row):
    parts = [row[:, k * 128:(k + 1) * 128] for k in range(D // 128)]
    return jnp.concatenate(parts + [jnp.zeros((8 - D // 128, 128), f32)], axis=0)


def unfold_row(x):
    return jnp.concatenate([x[k:k + 1] for k in range(D // 128)], axis=1)


def rms(v):
    r = lax.rsqrt(jnp.mean(v * v, axis=-1, keepdims=True) + eps)
    return v * r, r


def norm_back(y, r, pushed):
    return r * (pushed - y * jnp.mean(pushed * y, axis=-1, keepdims=True))


def gelu(u):
    c = math.sqrt(2.0 / math.pi)
    t = jnp.tanh(c * (u + 0.044715 * u * u * u))
    return 0.5 * u * (1.0 + t), 0.5 * (1.0 + t) + 0.5 * u * (1.0 - t * t) * c * (1.0 + 3 * 0.044715 * u * u)


def expand(x):
    col = iota(x.shape, 1) // HEAD
    return jnp.concatenate([jnp.where(col == j, x, 0) for j in range(PER)], axis=0)


def collapse(x, rows):
    out = 0
    for j in range(PER):
        part = x[j * rows:(j + 1) * rows]
        out = out + jnp.where(iota(part.shape, 1) // HEAD == j, part, 0)
    return out


def per_head(x, m, rows):
    col = iota((rows, WIDE), 1) // HEAD
    out = jnp.where(col == 0, x[:, PER * m:PER * m + 1], 0)
    for j in range(1, PER):
        out = jnp.where(col == j, x[:, PER * m + j:PER * m + j + 1], out)
    return out


def to_pairs(x):
    n = x.shape[0]
    wide = jnp.broadcast_to(x[:, None, :], (n, WIN, 128)).reshape(n * WIN, 128)
    wide = jnp.where(iota(wide.shape, 1) % WIN == iota(wide.shape, 0) % WIN, wide, 0.0)
    return exact(wide, (iota((128, 128), 0) // WIN == iota((128, 128), 1)).astype(f32))


def to_windows(x):
    wide = exact(x, (iota((128, 128), 0) == iota((128, 128), 1) // WIN).astype(f32))
    wide = jnp.where(iota(wide.shape, 1) % WIN == iota(wide.shape, 0) % WIN, wide, 0.0)
    return jnp.sum(wide.reshape(-1, WIN, 128), axis=1)


def put(src, dst, ssem, rsem, where):
    return pltpu.make_async_remote_copy(src_ref=src, dst_ref=dst, send_sem=ssem, recv_sem=rsem, device_id=where, device_id_type=MESH)


def flips(m):
    return (m + 2) % 4, m + 1 - 2 * (m % 2)


def merge(ca, la, cb, lb):
    top = jnp.maximum(la, lb)
    ea, eb = jnp.exp(la - top), jnp.exp(lb - top)
    total = ea + eb
    wa, wb = ea / total, eb / total
    n = la.shape[0]
    return [ca[m].astype(f32) * per_head(wa, m, n) + cb[m].astype(f32) * per_head(wb, m, n) for m in range(4)], top + jnp.log(total)


def blocks(ref):
    return [ref[m // 2, :, WIDE * (m % 2):WIDE * (m % 2 + 1)] for m in range(4)]


def fill(ref, values):
    for m in range(4):
        ref[m // 2, :, WIDE * (m % 2):WIDE * (m % 2 + 1)] = values[m].astype(ref.dtype)


def loop(first, end, body):
    whole = (end - first) // UNROLL

    def some(j, _):
        for i in range(UNROLL):
            body(first + j * UNROLL + i)
        return 0

    lax.fori_loop(0, whole, some, 0)
    for k in range(first + whole * UNROLL, end):
        body(k)


class Spread:
    def __init__(self, dst, sems, wide=False, early=False):
        self.dst, self.wide, self.early = dst, wide, early
        self.groups = dst.shape[1] if wide else dst.shape[0]
        self.lines = self.groups // 2
        self.snd, self.rz, self.ry, self.rx, self.rc, self.rq = (tuple(sems) + (None,) * 4)[:6]
        self.d, self.m = lax.axis_index("dp"), lax.axis_index("mp")
        self.o, self.i = self.d // 2, self.d % 2
        self.dy = self.d + 1 - 2 * self.i
        self.xm, self.cm = flips(self.m)

    def near(self, k):
        return (self.o + self.lines - k) % self.lines * 2 + self.i

    def far(self, k):
        return (self.o + self.lines - k) % self.lines * 2 + 1 - self.i

    def at(self, mm, dd):
        return self.dst.at[mm, dd] if self.wide else self.dst.at[dd]

    def send(self, mm, dd, way, sem, where):
        put(self.at(mm, dd), self.at(mm, dd), self.snd.at[way], sem, where).start()

    def got(self, mm, dd, sem):
        put(self.at(mm, dd), self.at(mm, dd), self.snd.at[0], sem, (self.d, self.xm)).wait_recv()

    def over(self, mm, k, sems):
        self.send(mm, self.near(k), 1, sems.at[k], (self.dy, self.m))

    def mates(self, dd, j):
        if self.wide:
            if j is not None:
                self.send(self.m, dd, 2, self.rx.at[j], (self.d, self.xm))
            self.send(self.m, dd, 3, self.rc.at[0], (self.d, self.cm))

    def own(self):
        for k in range(1, self.lines):
            self.send(self.m, self.d, 0, self.rz.at[k], ((self.o + k) % self.lines * 2 + self.i, self.m))
        self.over(self.m, 0, self.ry)
        self.mates(self.d, 0)

    def arrive(self, k):
        dd = self.near(k)
        self.got(self.m, dd, self.rz.at[k])
        if self.early:
            self.mates(dd, k)
            self.over(self.m, k, self.ry)
        else:
            self.over(self.m, k, self.ry)
            self.mates(dd, k)

    def across(self, k):
        dd = self.far(k)
        self.got(self.m, dd, self.ry.at[k])
        self.mates(dd, None if self.early else self.lines + k)

    def relay(self, j):
        dd = self.near(j) if j < self.lines else self.far(j - self.lines)
        self.got(self.xm, dd, self.rx.at[j])
        self.send(self.xm, dd, 4, self.rc.at[1], (self.d, self.cm))
        if self.early:
            self.over(self.xm, j, self.rq)

    def around(self, k):
        dd = self.far(k)
        self.got(self.xm, dd, self.rq.at[k])
        self.send(self.xm, dd, 4, self.rc.at[1], (self.d, self.cm))

    def events(self, start, pace):
        n, do = self.lines, functools.partial
        out = [(start + pace * k, do(self.arrive, k)) for k in range(1, n)]
        out += [(start + pace * (k + 1) + 1, do(self.across, k)) for k in range(n)]
        if self.early:
            out += [(start + 2 * pace * k + 3, do(self.relay, k)) for k in range(n)]
            out += [(start + 2 * pace * (k + 1) + 5, do(self.around, k)) for k in range(n)]
        elif self.wide:
            out += [(start + 2 * pace * j + 3, do(self.relay, j)) for j in range(2 * n)]
        return out

    def close(self):
        xcm = (self.cm + 2) % 4
        for sem, mm in ((0, self.cm), (1, xcm)):
            put(self.dst.at[mm], self.dst.at[mm], self.snd.at[0], self.rc.at[sem], (self.d, self.cm)).wait_recv()

    def sent(self):
        def done(way, pieces):
            ref = self.dst.at[0, pl.ds(0, pieces)] if self.wide else self.dst.at[pl.ds(0, pieces)]
            put(ref, ref, self.snd.at[way], self.rz.at[0], (self.d, self.cm)).wait_send()
        done(0, self.lines - 1)
        done(1, self.groups if self.early else self.lines)
        if self.wide:
            done(2, self.lines if self.early else self.groups)
            done(3, self.groups)
            done(4, self.groups)


class Reduce:
    def __init__(self, r, yb, ys, z, sems):
        self.lines, self.r, self.yb, self.ys, self.z = r.shape[0] // 2, r, yb, ys, z
        self.snd, self.yrec, self.zrec = sems
        self.d, self.m = lax.axis_index("dp"), lax.axis_index("mp")
        self.o, self.i = self.d // 2, self.d % 2
        self.order = list(range(1, self.lines)) + [0]

    def fill(self, value):
        groups, rows = self.r.shape[0], self.r.shape[1]
        for g in range(groups):
            self.r[g] = value[g * rows:(g + 1) * rows].astype(bf16)

    def target(self, k):
        return (self.o + k) % self.lines

    def over(self, k):
        return put(self.r.at[2 * self.target(k) + 1 - self.i], self.yb.at[k], self.snd.at[0], self.yrec.at[k], (self.d + 1 - 2 * self.i, self.m))

    def straight(self, k):
        return put(self.ys.at[k], self.z.at[k - 1], self.snd.at[1], self.zrec.at[k - 1], (self.target(k) * 2 + self.i, self.m))

    def start(self):
        for k in self.order:
            self.over(k).start()

    def fold(self, k):
        self.over(k).wait_recv()
        self.ys[k] = (self.r[2 * self.target(k) + self.i].astype(f32) + self.yb[k].astype(f32)).astype(bf16)
        if k:
            self.straight(k).start()

    def events(self):
        return [functools.partial(self.fold, k) for k in self.order]

    def finish(self):
        out = self.ys[0].astype(f32)
        for k in range(1, self.lines):
            self.straight(k).wait_recv()
            out = out + self.z[k - 1].astype(f32)
        for way, ref in ((0, self.r.at[pl.ds(0, self.lines)]), (1, self.ys.at[pl.ds(0, self.lines - 1)])):
            put(ref, ref, self.snd.at[way], self.zrec.at[0], (self.d, self.m)).wait_send()
        return out


class Queue:
    def __init__(self, items):
        self.items = list(items)

    def take(self, gaps):
        for _ in range(-(-len(self.items) // gaps)):
            self.items.pop(0)()


def layer_kernel(groups, weight, names, *refs):
    R = dict(zip(names, refs))

    class N:
        pass

    r = N()
    for key, ref in R.items():
        setattr(r, key, ref)
    micros, pairs = r.x0.shape[0], r.x0.shape[1]
    n = micros * pairs
    wins = pairs // WIN
    rows = r.sv.shape[0]
    tiles = r.enc.shape[0] // micros
    span = tiles * TILE
    steps = tiles + wins - 1
    total = 4 * groups
    lines = groups // 2
    d, m = lax.axis_index("dp"), lax.axis_index("mp")
    me = d * 4 + m
    xm, cm = flips(m)
    base = m * span

    for u in range(micros):
        for t in range(tiles):
            pltpu.make_async_copy(r.enc_hbm.at[u, pl.ds(base + t * TILE, TILE), :], r.enc.at[u * tiles + t], r.esem.at[u]).start()

    barrier = pltpu.get_barrier_semaphore()

    def hello(j, _):
        to = (me + j) % total
        pl.semaphore_signal(barrier, inc=1, device_id=(to // 4, to % 4), device_id_type=MESH)
        return 0

    lax.fori_loop(1, total, hello, 0)

    eye = (iota((rows, rows), 0) == iota((rows, rows), 1)).astype(bf16)

    def turned(x):
        return dot(eye, x, 1, 1).astype(bf16)

    def scaled(g, x):
        return (to_column(g.astype(f32)) * x.astype(f32)).astype(bf16)

    r.a1[m, d, :, 0:192] = scaled(r.g1[...], r.sv[...])
    r.a1[m, d, :, 192:384] = turned(r.so[...])
    r.a2[m, d, :, 0:192] = scaled(r.g2[...], r.wq[...])
    r.a2[m, d, :, 192:384] = r.wk[...]
    pl.semaphore_wait(barrier, total - 1)
    A1 = Spread(r.a1, (r.sa1, r.za1, r.ya1, r.xa1, r.ca1), wide=True)
    A2 = Spread(r.a2, (r.sa2, r.za2, r.ya2, r.xa2, r.ca2, r.qa2), wide=True, early=True)
    A3 = Spread(r.a3, (r.sa3, r.za3, r.ya3, r.xa3, r.ca3), wide=True)
    B1 = Spread(r.b1, (r.sb1, r.zb1, r.yb1))
    B2 = Spread(r.b2, (r.sb2, r.zb2, r.yb2))
    F = Spread(r.fd, (r.sf, r.zf, r.yf))
    A1.own()
    A2.own()
    r.b1[d] = scaled(r.g3[...], r.fi[...])
    r.a3[m, d, :, 0:192] = r.wv[...]
    r.a3[m, d, :, 192:384] = turned(r.co[...])
    r.b2[d] = r.fo[...]
    direction = r.dir1[...].astype(f32)
    own_dir = jnp.sum(jnp.where(iota((rows, D), 1) == d * rows + iota((rows, D), 0), direction, 0.0), axis=1, keepdims=True)
    r.fd[d] = fold_row(jnp.sum(own_dir * r.fo[...].astype(f32), axis=0, keepdims=True))

    for u in range(micros):
        def running(p, at, u=u):
            at = at + r.lens[u, 0, p]
            r.ends[u, p] = at
            return at
        lax.fori_loop(0, pairs, running, jnp.int32(0))
        w0 = jnp.int32(0)
        for w in range(wins):
            w0 = w0 + jnp.where(r.ends[u, WIN * w + WIN - 1] <= base, 1, 0)

        def stair(k, carry, u=u):
            t, w, live, pt, pw = carry
            r.tk[u, k] = t
            r.wk_[u, k] = w
            r.at[u, k] = jnp.where(live == 1, base + t * TILE, -(1 << 20))
            r.keepw[u, k] = jnp.where(w == pw, 1.0, 0.0)
            r.keept[u, k] = jnp.where(t == pt, 1.0, 0.0)
            wend, tend = r.ends[u, WIN * w + WIN - 1], base + (t + 1) * TILE
            nt = t + jnp.where(wend >= tend, 1, 0)
            nw = w + jnp.where(wend <= tend, 1, 0)
            on = live * jnp.where(nt < tiles, 1, 0)
            return jnp.where(on == 1, nt, t), jnp.minimum(jnp.where(on == 1, nw, w), wins - 1), on, t, w

        lax.fori_loop(0, steps, stair, (jnp.int32(0), jnp.minimum(w0, wins - 1), jnp.int32(1), jnp.int32(-1), jnp.int32(-1)))

        def last(table, out, count, u=u):
            def one(i, _):
                def scan(k, best):
                    return jnp.where(table[u, k] == i, k, best)
                out[u, i] = lax.fori_loop(0, steps, scan, jnp.int32(-1))
                return 0
            lax.fori_loop(0, count, one, 0)

        last(r.wk_, r.lw, wins)
        last(r.tk, r.lt, tiles)
    lens = jnp.concatenate([r.lensv[u].astype(f32) for u in range(micros)] + [jnp.zeros((8 - micros, pairs), f32)], axis=0)
    for w in range(wins):
        lane = iota((pairs, 128), 1)
        pair = WIN * w + lane % WIN
        stop = exact(lens, ((iota((pairs, 128), 0) <= pair) & (lane < COLS)).astype(f32))
        start = exact(lens, ((iota((pairs, 128), 0) < pair) & (lane < COLS)).astype(f32))
        for u in range(micros):
            r.hi[u, w] = stop[u:u + 1]
            r.lo[u, w] = start[u:u + 1]

    everyone = groups * pairs
    for g in range(groups):
        r.slotr[g:g + 1, :] = jnp.concatenate([r.slot[u:u + 1, g * pairs:(g + 1) * pairs] + u * everyone for u in range(micros)], axis=1)
    square = iota((n, n), 0) == iota((n, n), 1)
    slotc = jnp.sum(jnp.where(square, r.slotr[pl.ds(d, 1), :], 0), axis=1, keepdims=True)
    keyc = slotc // CAND

    for u in range(micros):
        part = r.enc.at[pl.ds(u * tiles, tiles)]
        pltpu.make_async_copy(part, part, r.esem.at[u]).wait()

    urgent = A1.events(2.0, 1.5) + A2.events(3.5, 1.5)
    last_one = max(t for t, _ in urgent)
    later = [(6.0, B1.own), (7.0, F.own), (9.0, A3.own)] + B1.events(9.0, 3.0) + F.events(11.0, 3.0) + A3.events(12.0, 2.0)
    events = sorted(urgent + later, key=lambda e: e[0])
    for t, e in events:
        if t <= last_one:
            e()
    A1.close()
    A2.close()
    queue = Queue(e for t, e in events if t > last_one)

    def weight_of(ref, k, c0):
        return ref[k, :, :, c0:c0 + WIDE].reshape(D, WIDE)

    G0 = Reduce(r.r0, r.yr0, r.ys0, r.z0, (r.snd0, r.yrec0, r.zrec0))
    GV = Reduce(r.r2, r.yr2, r.ys2, r.z2, (r.snd2, r.yrec2, r.zrec2))
    def halve(src, buf, mid, fin, ss, rs):
        xcm = (cm + 2) % 4
        near = [put(src.at[cm], buf.at[0], ss.at[0], rs.at[0], (d, cm)), put(src.at[xcm], buf.at[1], ss.at[1], rs.at[1], (d, cm))]
        far = put(mid, fin, ss.at[2], rs.at[2], (d, xm))

        def one():
            for c in near:
                c.start()

        def two():
            for c in near:
                c.wait()
            mid[...] = (src[xm].astype(f32) + buf[1].astype(f32)).astype(bf16)
            far.start()

        def three():
            far.wait()
            return src[m].astype(f32) + buf[0].astype(f32) + fin[...].astype(f32)

        return one, two, three

    chunks = ((0, 7), (7, 13), (13, steps))

    def attention(chain, acc):
        r.chain, r.acc = chain, acc
        x0 = r.x0[...].reshape(n, D).astype(f32)
        y1b = rms(x0)[0].astype(bf16)
        x1 = x0
        for k in range(4):
            v1 = dot(y1b, weight_of(r.a1, k, 0)).astype(bf16)
            r.v1[k] = v1
            x1 = x1 + dot(v1, weight_of(r.a1, k, 192), 1, 1)
        r.x1[...] = x1
        y2b = rms(x1)[0].astype(bf16)

        def fill_windows(k, value):
            for j in range(PER):
                h = PER * k + j
                r.chain[0:micros * wins, h * WIN:(h + 1) * WIN, :] = value[j * n:(j + 1) * n].reshape(micros * wins, WIN, D)

        gap = jnp.zeros((micros, wins, 128 - COLS, D), bf16)
        for k in range(4):
            q = dot(y2b, weight_of(r.a2, k, 0)).astype(bf16)
            r.q[k] = q
            fill_windows(k, dot(expand(q), weight_of(r.a2, k, 192), 1, 1))
        r.qu[:, :, 0:COLS, :] = r.chain[0:micros * wins].astype(bf16).reshape(micros, wins, COLS, D)
        r.qu[:, :, COLS:128, :] = gap
        r.qu[:, :, 128 + COLS:256, :] = gap

        gaps = 2 * micros * len(chunks)

        def tile_rows(u, k):
            return r.enc[u * tiles + r.tk[u, k]]

        line = iota((TILE, 128), 0).astype(f32)
        for u in range(micros):
            def scores(k, u=u):
                w = r.wk_[u, k]
                s = dot(tile_rows(u, k), r.qu[u, w, 0:128, :], 1, 1)
                at = line + r.at[u, k].astype(f32)
                s = jnp.where((at >= r.lo[u, w]) & (at < r.hi[u, w]), s, FAR)
                high = s.astype(bf16)
                r.da[u, k, :, 0:128] = high
                r.da[u, k, :, 128:256] = (s - high.astype(f32)).astype(bf16)
                r.sm[k] = jnp.max(s, axis=0, keepdims=True)

            for a, b in chunks:
                loop(a, b, scores)
                queue.take(gaps)
                gaps -= 1
            for w in range(wins):
                top = jnp.full((1, 128), FAR, f32)
                for k in range(steps):
                    top = jnp.where(jnp.full((1, 128), r.wk_[u, k]) == w, jnp.maximum(top, r.sm[k]), top)
                r.mw[u, w] = top

            def weights(k, u=u):
                w = r.wk_[u, k]
                s = r.da[u, k, :, 0:128].astype(f32) + r.da[u, k, :, 128:256].astype(f32)
                p = jnp.where(s > 0.5 * FAR, jnp.exp(s - r.mw[u, w]), 0.0)
                r.sm[k] = jnp.sum(p, axis=0, keepdims=True)
                low = p.astype(bf16)
                r.da[u, k, :, 128:256] = low
                acc = dot(low, tile_rows(u, k), 0, 0)[0:COLS] + r.acc[0:COLS] * r.keepw[u, k]
                r.acc[0:COLS] = acc
                r.chain[k] = acc

            r.acc[...] = jnp.zeros_like(r.acc)
            for a, b in chunks:
                loop(a, b, weights)
                queue.take(gaps)
                gaps -= 1
            for w in range(wins):
                tot = jnp.zeros((1, 128), f32)
                for k in range(steps):
                    tot = jnp.where(jnp.full((1, 128), r.wk_[u, k]) == w, tot + r.sm[k], tot)
                r.lw_[u, w] = tot
            inv = to_pairs(r.lw_[u].reshape(wins, 128))
            inv = jnp.where(inv > 0.0, 1.0 / jnp.where(inv > 0.0, inv, 1.0), 0.0)
            for h in range(HEADS):
                parts = []
                for w in range(wins):
                    k = r.lw[u, w]
                    part = r.chain[jnp.maximum(k, 0), h * WIN:(h + 1) * WIN, :]
                    scale = inv[w * WIN:(w + 1) * WIN, h:h + 1]
                    parts.append(jnp.where(scale > 0.0, part * scale, 0.0))
                r.c[h, u * pairs:(u + 1) * pairs, :] = jnp.concatenate(parts, axis=0).astype(bf16)
        while queue.items:
            queue.take(1)
        A3.close()
        B2.own()
        mx = to_pairs(r.mw[...].reshape(micros * wins, 128))
        lx = to_pairs(r.lw_[...].reshape(micros * wins, 128))
        some = lx > 0.0
        lse_own = jnp.where(some, mx + jnp.log(jnp.where(some, lx, 1.0)), FAR)
        r.mx[...] = mx
        r.lown[...] = lse_own
        own = []
        for k in range(4):
            ctx = collapse(dot(r.c[PER * k:PER * (k + 1)].reshape(PER * n, D), weight_of(r.a3, k, 0)), n)
            own.append(ctx)
        fill(r.csend, own)
        hop = [put(r.csend, r.cbuf0, r.csem.at[0], r.crec.at[0], (d, cm)), put(r.lown, r.lbuf.at[0], r.csem.at[1], r.crec.at[1], (d, cm))]
        for c in hop:
            c.start()
        fd = r.fd[0]
        for g in range(1, groups):
            fd = fd + r.fd[g]
        fd = unfold_row(fd)
        for c in hop:
            c.wait()
        both, lse = merge(own, lse_own, blocks(r.cbuf0), r.lbuf[0])
        fill(r.cmid, both)
        r.lmid[...] = lse
        hop = [put(r.cmid, r.cbuf1, r.csem.at[2], r.crec.at[2], (d, xm)), put(r.lmid, r.lbuf.at[1], r.csem.at[3], r.crec.at[3], (d, xm))]
        for c in hop:
            c.start()
        for c in hop:
            c.wait()
        both, lse = merge(both, lse, blocks(r.cbuf1), r.lbuf[1])
        r.lse[...] = lse
        x2 = r.x1[...]
        for k in range(4):
            low = both[k].astype(bf16)
            r.ctx[k] = low
            x2 = x2 + dot(low, weight_of(r.a3, k, 192), 1, 1)
        ffi = r.b1[...].reshape(D, D)
        y3, r3 = rms(x2)
        y3b = y3.astype(bf16)
        act, slope = gelu(dot(y3b, ffi))
        hid = act.astype(bf16)
        hidf = hid.astype(f32)
        score = jnp.sum(hidf * fd, axis=1, keepdims=True) + jnp.where(m == 0, jnp.sum(x2 * direction, axis=1, keepdims=True), 0.0)
        rel = jnp.concatenate([r.rel[u:u + 1, :] for u in range(micros)], axis=1)
        which = iota((8, n), 0)
        r.msgs[0] = jnp.where(which == 0, to_row(score), jnp.where(which == 1, rel, 0.0))

        def tell(j, _):
            to = (me + j) % total
            put(r.msgs.at[0], r.msgs.at[total - j], r.msem.at[0], r.msem.at[1], (to // 4, to % 4)).start()
            return 0

        lax.fori_loop(1, total, tell, 0)
        r.hid[...] = hid
        r.x3[...] = x2.reshape(micros, pairs, D)

        heard = r.msgs.at[pl.ds(1, total - 1)]
        put(heard, heard, r.msem.at[0], r.msem.at[1], (d, cm)).wait()
        lane = iota((1, n), 1)

        def rows_of(g):
            four = [r.msgs[(4 * g + k - me + total) % total] for k in range(4)]
            s = (four[0] + four[1] + four[2] + four[3])[0:1]
            slot = (lane // pairs) * everyone + g * pairs + lane % pairs
            mine = r.slotr[pl.ds(g, 1), :]
            return s, four[0][1:2], mine // CAND == keyc, mine == slotc, slot // CAND == keyc, slot == slotc

        def tops(g, carry):
            a, b, own, rown = carry
            s, rel, same, mine, rsame, rmine = rows_of(g)
            return (jnp.maximum(a, jnp.where(same, s, FAR)), jnp.maximum(b, jnp.where(rsame, rel, FAR)),
                    own + jnp.where(mine, s, 0.0), rown + jnp.where(rmine, rel, 0.0))

        z = jnp.zeros((n, n), f32)
        far = jnp.full((n, n), FAR, f32)
        a, b, sown, rown = lax.fori_loop(0, groups, tops, (far, far, z, z), unroll=groups <= 8)
        a, b = jnp.max(a, axis=1, keepdims=True), jnp.max(b, axis=1, keepdims=True)
        sown, rown = jnp.sum(sown, axis=1, keepdims=True), jnp.sum(rown, axis=1, keepdims=True)

        def sums(g, carry):
            s, rel, same, _, rsame, _ = rows_of(g)
            return (carry[0] + jnp.where(same, jnp.exp(s - a), 0.0), carry[1] + jnp.where(rsame, jnp.exp(rel - b), 0.0))

        sa, sb = lax.fori_loop(0, groups, sums, (z, z), unroll=groups <= 8)
        dscore = weight * (jnp.exp(sown - a) / jnp.sum(sa, axis=1, keepdims=True) - jnp.exp(rown - b) / jnp.sum(sb, axis=1, keepdims=True))
        du = (slope * dscore * fd).astype(bf16)
        dn3p = dot(du, ffi, 1, 1)
        r.nmid[0] = dn3p.astype(bf16)
        nhop = put(r.nmid.at[0], r.nbuf.at[0], r.nsem.at[0], r.nrec.at[0], (d, cm))
        nhop.start()
        r.hsum[0] = fold_row(jnp.sum(hidf * dscore, axis=0, keepdims=True))

        def scatter(j, _):
            to = (d + j) % groups
            put(r.hsum.at[0], r.hsum.at[groups - j], r.hsem.at[0], r.hsem.at[1], (to, m)).start()
            return 0

        nhop.wait()
        part = dn3p + r.nbuf[0].astype(f32)
        r.nmid[1] = part.astype(bf16)
        nhop = put(r.nmid.at[1], r.nbuf.at[1], r.nsem.at[1], r.nrec.at[1], (d, xm))
        nhop.start()
        lax.fori_loop(1, groups, scatter, 0)
        gff = dot(y3b, du, 0, 0)
        nhop.wait()
        dn3 = part + r.nbuf[1].astype(f32)
        dx2 = dscore * direction + norm_back(y3, r3, dn3)
        r.dx2[...] = dx2
        gc = dx2.astype(bf16)
        delta = jnp.zeros((n, 128), f32)
        for k in range(4):
            dctx = dot(gc, weight_of(r.a3, k, 192)).astype(bf16)
            r.dctx[k] = dctx
            pick = (iota((WIDE, 128), 0) // HEAD + PER * k == iota((WIDE, 128), 1)).astype(f32)
            delta = delta + exact(dctx.astype(f32) * both[k], pick)
        ones = jnp.ones((n, 64), bf16)
        G0.fill(jnp.concatenate([gff, dot(gc, r.ctx[m], 0, 0), dot((dn3 * y3).astype(bf16), ones, 0, 0)], axis=1))
        G0.start()
        r.alpha[...] = to_windows(jnp.exp(jnp.minimum(r.mx[...] - lse, 1.0))).reshape(r.alpha.shape)
        r.delta[...] = to_windows(delta).reshape(r.delta.shape)
        share = jnp.exp(jnp.minimum(r.lown[...] - lse, 1.0))
        for k in range(4):
            dctx = expand(r.dctx[k])
            fill_windows(k, dot(dctx, weight_of(r.a3, k, 0), 1, 1))
            spread = jnp.concatenate([dctx[j * n:(j + 1) * n] * share[:, PER * k + j:PER * k + j + 1].astype(bf16) for j in range(PER)], axis=0)
            r.g[k] = dot(r.c[PER * k:PER * (k + 1)].reshape(PER * n, D), spread, 0, 0).astype(bf16)
        r.qu[:, :, 128:128 + COLS, :] = r.chain[0:micros * wins].astype(bf16).reshape(micros, wins, COLS, D)

        v_one, v_two, v_three = halve(r.g, r.gvb, r.gvm, r.gvf, r.vsem, r.vrec)
        v_one()

        def value_out():
            GV.fill(jnp.concatenate([v_three(), jnp.zeros((D, 64), f32)], axis=1))
            GV.start()

        queue.items = [v_two] + G0.events() + [value_out] + [e for _, e in sorted(B2.events(0.0, 1.0), key=lambda e: e[0])] + GV.events()
        gaps = micros * len(chunks) + 3

        def back(k, u):
            w = r.wk_[u, k]
            tile = tile_rows(u, k)
            da = dot(tile, r.qu[u, w, 128:256, :], 1, 1)
            a = r.da[u, k, :, 128:256].astype(f32) * r.alpha[u, w]
            ds = (a * (da - r.delta[u, w])).astype(bf16)
            r.da[u, k, :, 0:128] = ds
            r.da[u, k, :, 128:256] = a.astype(bf16)
            acc = dot(ds, tile, 0, 0)[0:COLS] + r.acc[0:COLS] * r.keepw[u, k]
            r.acc[0:COLS] = acc
            r.chain[k] = acc

        for u in range(micros):
            r.acc[...] = jnp.zeros_like(r.acc)
            for a, b in chunks:
                loop(a, b, lambda k, u=u: back(k, u))
                queue.take(gaps)
                gaps -= 1
            for h in range(HEADS):
                parts = []
                for w in range(wins):
                    k = r.lw[u, w]
                    parts.append(jnp.where(jnp.full((WIN, D), k) >= 0, r.chain[jnp.maximum(k, 0), h * WIN:(h + 1) * WIN, :], 0.0))
                r.c[h, u * pairs:(u + 1) * pairs, :] = jnp.concatenate(parts, axis=0).astype(bf16)

    pl.run_scoped(attention, pltpu.VMEM((steps, COLS, D), f32), pltpu.VMEM((128, D), f32))

    def rest_of_it(r1, ys1, full, out):
        r.r1, r.ys1, r.full, r.out = r1, ys1, full, out
        G1 = Reduce(r.r1, r.yr1, r.ys1, r.z1, (r.snd1, r.yrec1, r.zrec1))
        part = [collapse(dot(r.c[PER * k:PER * (k + 1)].reshape(PER * n, D), weight_of(r.a2, k, 192)), n) for k in range(4)]
        fill(r.csend, part)
        hop = put(r.csend, r.cbuf0, r.qsem.at[0], r.qrec.at[0], (d, cm))
        hop.start()
        for k in range(4):
            r.g[k] = dot(r.c[PER * k:PER * (k + 1)].reshape(PER * n, D), expand(r.q[k]), 0, 0).astype(bf16)
        k_one, k_two, k_three = halve(r.g, r.gkb, r.gvm, r.gkf, r.ksem, r.krec)
        hop.wait()
        part = [x + y.astype(f32) for x, y in zip(part, blocks(r.cbuf0))]
        fill(r.cmid, part)
        hop = put(r.cmid, r.cbuf1, r.qsem.at[1], r.qrec.at[1], (d, xm))
        hop.start()
        k_one()
        while queue.items:
            queue.take(1)
        x3p = dot(r.hid[...], r.b2[...].reshape(D, D), 1, 1)
        r.nmid[0] = x3p.astype(bf16)
        xhop = put(r.nmid.at[0], r.nbuf.at[0], r.xsem.at[0], r.xrec.at[0], (d, cm))
        xhop.start()
        x1 = r.x1[...]
        y1, g1 = rms(r.x0[...].reshape(n, D).astype(f32))
        y2, g2 = rms(x1)
        k_two()
        hop.wait()
        dn2 = 0
        for k in range(4):
            dq = (part[k] + blocks(r.cbuf1)[k].astype(f32)).astype(bf16)
            r.dq[k] = dq
            dn2 = dn2 + dot(dq, weight_of(r.a2, k, 0), 1, 1)
        dx1 = r.dx2[...] + norm_back(y2, g2, dn2)
        gs = dx1.astype(bf16)
        dn1 = 0
        for k in range(4):
            dv = dot(gs, weight_of(r.a1, k, 192)).astype(bf16)
            r.dctx[k] = dv
            dn1 = dn1 + dot(dv, weight_of(r.a1, k, 0), 1, 1)
        r.dx0[...] = (dx1 + norm_back(y1, g1, dn1)).reshape(micros, pairs, D)
        ones = jnp.ones((n, 64), bf16)
        half_ones = jnp.where(iota((n, 64), 1) < 32, ones, 0)
        small = [dot(y1.astype(bf16), r.dctx[m], 0, 0), dot(gs, r.v1[m], 0, 0), dot(y2.astype(bf16), r.dq[m], 0, 0)]
        tail = dot((dn1 * y1).astype(bf16), half_ones, 0, 0) + dot((dn2 * y2).astype(bf16), ones - half_ones, 0, 0)
        G1.fill(jnp.concatenate(small + [k_three(), tail, jnp.zeros((D, 64), f32)], axis=1))
        G1.start()
        xhop.wait()
        x3p = x3p + r.nbuf[0].astype(f32)
        r.nmid[1] = x3p.astype(bf16)
        xhop = put(r.nmid.at[1], r.nbuf.at[1], r.xsem.at[1], r.xrec.at[1], (d, xm))
        xhop.start()
        queue.items += G1.events()
        gaps = micros * 4

        def rows_out(u, t, slot):
            return pltpu.make_async_copy(r.out.at[slot], r.de.at[u, pl.ds(t * TILE, TILE), :], r.osem.at[slot])

        for u in range(micros):
            if u == 0:
                r.full[...] = jnp.zeros_like(r.full)
            for a, b in ((0, 10), (10, steps)):
                loop(a, b, functools.partial(place, r, u))
                queue.take(gaps)
                gaps -= 1
            for t in range(tiles):
                slot = (u * tiles + t) % OUTS
                if u * tiles + t >= OUTS:
                    rows_out(u, t, slot).wait()
                k = jnp.maximum(r.lt[u, t], 0)
                r.out[slot] = r.enc[k]
                rows_out(u, t, slot).start()
                if t % 6 == 5:
                    queue.take(gaps)
                    gaps -= 1
        for slot in range(OUTS):
            rows_out(micros - 1, tiles - 1, slot).wait()
        while queue.items:
            queue.take(1)

        heard = r.hsum.at[pl.ds(1, groups - 1)]
        put(heard, heard, r.hsem.at[0], r.hsem.at[1], (d, cm)).wait()
        total_h = r.hsum[0]
        for g in range(1, groups):
            total_h = total_h + r.hsum[g]
        r.hs[...] = total_h
        xhop.wait()
        r.x3[...] = r.x3[...] + (x3p + r.nbuf[1].astype(f32)).reshape(micros, pairs, D)
        r.out0[...] = G0.finish()
        r.out2[...] = GV.finish()
        r.out1[...] = G1.finish()

    pl.run_scoped(rest_of_it, pltpu.VMEM((groups, rows, 896), bf16), pltpu.VMEM((lines, rows, 896), bf16), pltpu.VMEM((TILE, D), f32), pltpu.VMEM((OUTS, TILE, D), bf16))
    for part in (A1, A2, A3, B1, B2, F):
        part.sent()


def place(r, u, k):
    acc = dot(r.da[u, k], r.qu[u, r.wk_[u, k]]) + r.full[...] * r.keept[u, k]
    r.full[...] = acc
    r.enc[k] = acc.astype(bf16)


def layer(groups, weight, x0, encoded, lens, slot, rel, dir1, g1, g2, g3, sv, so, wq, wk, wv, co, fi, fo):
    micros, pairs = x0.shape[0], x0.shape[1]
    n, wins, rows, lines = micros * pairs, pairs // WIN, sv.shape[0], groups // 2
    span = encoded.shape[1] // 4
    tiles = span // TILE
    steps = tiles + wins - 1
    sd = jax.ShapeDtypeStruct
    any_, vm, sm = (pl.BlockSpec(memory_space=s) for s in (pl.ANY, pltpu.VMEM, pltpu.SMEM))
    S, V, M = pltpu.SemaphoreType.DMA, pltpu.VMEM, pltpu.SMEM
    ins = dict(x0=x0, enc_hbm=encoded, lens=lens, lensv=lens, slot=slot, rel=rel, dir1=dir1, g1=g1, g2=g2, g3=g3,
               sv=sv, so=so, wq=wq, wk=wk, wv=wv, co=co, fi=fi, fo=fo)
    places = dict(enc_hbm=any_, lens=sm)
    outs = dict(x3=sd((micros, pairs, D), f32), dx0=sd((micros, pairs, D), f32), de=sd((micros, span, D), bf16), hs=sd((8, 128), f32),
                out0=sd((rows, 1024), f32), out1=sd((rows, 896), f32), out2=sd((rows, 256), f32))
    places.update(de=any_)
    scratch = dict(
        enc=V((max(micros * tiles, steps), TILE, D), bf16), esem=S((micros,)),
        a1=V((4, groups, rows, 384), bf16), a2=V((4, groups, rows, 384), bf16), a3=V((4, groups, rows, 384), bf16),
        b1=V((groups, rows, D), bf16), b2=V((groups, rows, D), bf16), fd=V((groups, 8, 128), f32), hid=V((n, D), bf16),
        ends=M((micros, pairs), jnp.int32), tk=M((micros, steps), jnp.int32), wk_=M((micros, steps), jnp.int32), at=M((micros, steps), jnp.int32),
        keepw=M((micros, steps), f32), keept=M((micros, steps), f32), lw=M((micros, wins), jnp.int32), lt=M((micros, tiles), jnp.int32),
        lo=V((micros, wins, 1, 128), f32), hi=V((micros, wins, 1, 128), f32), slotr=V((groups, n), jnp.int32),
        x1=V((n, D), f32), v1=V((4, n, WIDE), bf16), q=V((4, n, WIDE), bf16), qu=V((micros, wins, 256, D), bf16), sm=V((steps, 1, 128), f32), mw=V((micros, wins, 1, 128), f32), lw_=V((micros, wins, 1, 128), f32),
        da=V((micros, steps, TILE, 256), bf16), c=V((HEADS, n, D), bf16), mx=V((n, 128), f32), lown=V((n, 128), f32), lse=V((n, 128), f32),
        csend=V((2, n, 384), bf16), cmid=V((2, n, 384), bf16), cbuf0=V((2, n, 384), bf16), cbuf1=V((2, n, 384), bf16), lmid=V((n, 128), f32), lbuf=V((2, n, 128), f32),
        csem=S((4,)), crec=S((4,)), ctx=V((4, n, WIDE), bf16), msgs=V((4 * groups, 8, n), f32), msem=S((2,)),
        xsem=S((2,)), xrec=S((2,)), nmid=V((2, n, D), bf16), nbuf=V((2, n, D), bf16), nsem=S((2,)), nrec=S((2,)),
        hsum=V((groups, 8, 128), f32), hsem=S((2,)), dx2=V((n, D), f32), dctx=V((4, n, WIDE), bf16), dq=V((4, n, WIDE), bf16),
        alpha=V((micros, wins, 1, 128), f32), delta=V((micros, wins, 1, 128), f32),
        g=V((4, D, WIDE), bf16), gvb=V((2, D, WIDE), bf16), gvm=V((D, WIDE), bf16), gvf=V((D, WIDE), bf16), vsem=S((3,)), vrec=S((3,)),
        gkb=V((2, D, WIDE), bf16), gkf=V((D, WIDE), bf16), ksem=S((3,)), krec=S((3,)), qsem=S((2,)), qrec=S((2,)),
        osem=S((OUTS,)),
    )
    for part in ("a1", "a2", "a3", "b1", "b2", "f"):
        scratch.update({"s" + part: S((5,)), "z" + part: S((lines,)), "y" + part: S((lines,))})
        if part[0] == "a":
            scratch.update({"x" + part: S((groups,)), "c" + part: S((2,)), "q" + part: S((lines,))})
    for tag, columns in (("0", 1024), ("1", 896), ("2", 256)):
        piece = lambda k: V((k, rows, columns), bf16)
        if tag != "1":
            scratch.update({"r" + tag: piece(groups), "ys" + tag: piece(lines)})
        scratch.update({"yr" + tag: piece(lines), "z" + tag: piece(lines - 1),
                        "snd" + tag: S((2,)), "yrec" + tag: S((lines,)), "zrec" + tag: S((lines - 1,))})
    names = tuple(ins) + tuple(outs) + tuple(scratch)
    return pl.pallas_call(
        functools.partial(layer_kernel, groups, weight, names),
        out_shape=tuple(outs.values()),
        in_specs=[places.get(k, vm) for k in ins], out_specs=[places.get(k, vm) for k in outs],
        scratch_shapes=list(scratch.values()),
        compiler_params=pltpu.CompilerParams(collective_id=0, has_side_effects=True, vmem_limit_bytes=VMEM),
        name="decoder_layer",
    )(*ins.values())


def outputs_kernel(dir_ref, hs, out0, out1, out2, g1, g2, g3, x3, dx0, de,
                   g_self, g_cross, g_ff, self_value, self_out, query, key, value, cross_out, ff_in, ff_out, x3_out, dx0_out, de_out, room, sem):
    parts = de.shape[1] // 768
    every = [(u, pl.ds(k * 768, 768), u * parts + k) for u in range(de.shape[0]) for k in range(parts)]
    loads = [pltpu.make_async_copy(de.at[u, at], room.at[k], sem.at[0, k]) for u, at, k in every]
    stores = [pltpu.make_async_copy(room.at[k], de_out.at[u, at], sem.at[1, k]) for u, at, k in every]
    for c in loads:
        c.start()
    rows = out0.shape[0]
    columns = [to_column(g[...].astype(f32)) for g in (g1, g2, g3)]
    g_self[...] = to_row(out1[:, 768:769] / columns[0])
    g_cross[...] = to_row(out1[:, 800:801] / columns[1])
    g_ff[...] = to_row(out0[:, 960:961] / columns[2])
    self_value[...] = out1[:, 0:192] * columns[0]
    self_out[...] = out1[:, 192:384].T
    query[...] = out1[:, 384:576] * columns[1]
    key[...] = out1[:, 576:768]
    value[...] = out2[:, 0:192]
    cross_out[...] = out0[:, 768:960].T
    ff_in[...] = out0[:, 0:768] * columns[2]
    mine = iota((rows, D), 1) == lax.axis_index("dp") * rows + iota((rows, D), 0)
    own_dir = jnp.sum(jnp.where(mine, dir_ref[...].astype(f32), 0.0), axis=1, keepdims=True)
    ff_out[...] = own_dir * unfold_row(hs[...])
    x3_out[...] = x3[...]
    dx0_out[...] = dx0[...]
    for c, back in zip(loads, stores):
        c.wait()
        back.start()
    for c in stores:
        c.wait()


def outputs(dir1, hs, out0, out1, out2, g1, g2, g3, x3, dx0, de):
    rows, count = out0.shape[0], de.shape[0] * de.shape[1] // 768
    sd = jax.ShapeDtypeStruct
    tall, flat = sd((rows, WIDE), f32), sd((WIDE, rows), f32)
    any_, vm = (pl.BlockSpec(memory_space=s) for s in (pl.ANY, pltpu.VMEM))
    return pl.pallas_call(
        outputs_kernel,
        out_shape=(sd((1, rows), f32),) * 3 + (tall, flat, tall, tall, tall, flat, sd((rows, D), f32), sd((rows, D), f32),
                                               sd(x3.shape, f32), sd(x3.shape, f32), sd(de.shape, bf16)),
        in_specs=[vm] * 10 + [any_], out_specs=[vm] * 13 + [any_],
        scratch_shapes=[pltpu.VMEM((count, 768, D), bf16), pltpu.SemaphoreType.DMA((2, count))],
        compiler_params=pltpu.CompilerParams(vmem_limit_bytes=32 << 20),
        name="outputs",
    )(dir1, hs, out0, out1, out2, g1, g2, g3, x3, dx0, de)


def shards(dec_in, encoded, seg_lengths, pair_slot, relevance, score_dir, gain_self, gain_cross, gain_ff,
           self_value, self_out, cross_query, cross_key, cross_value, cross_out, ff_in, ff_out):
    groups = lax.axis_size("dp")
    gains = [g.reshape(1, -1) for g in (gain_self, gain_cross, gain_ff)]
    dir1 = score_dir.reshape(1, D)
    x3, dx0, d_encoded, hs, out0, out1, out2 = layer(
        groups, CAND * math.sqrt(D), dec_in, encoded, seg_lengths, pair_slot, relevance, dir1, *gains,
        self_value, self_out, cross_query, cross_key, cross_value, cross_out, ff_in, ff_out.T)
    g1, g2, g3, *weights, x3, dx0, d_encoded = outputs(dir1, hs, out0, out1, out2, *gains, x3, dx0, d_encoded)
    weights[-1] = weights[-1].T
    return (x3, dx0, d_encoded, g1.reshape(-1), g2.reshape(-1), g3.reshape(-1), *weights)


def solution(mesh):
    in_specs = (
        P(None, "dp", None),
        P(None, "dp", None),
        P(None, "dp", None),
        P(),
        P(None, "dp"),
        P(),
        P("dp"),
        P("dp"),
        P("dp"),
        P("dp", "mp"),
        P("mp", "dp"),
        P("dp", "mp"),
        P("dp", "mp"),
        P("dp", "mp"),
        P("mp", "dp"),
        P("dp", "mp"),
        P("mp", "dp"),
    )
    out_specs = (
        P(None, "dp", None),
        P(None, "dp", None),
        P(None, ("dp", "mp"), None),
        P("dp"),
        P("dp"),
        P("dp"),
        P("dp", "mp"),
        P("mp", "dp"),
        P("dp", "mp"),
        P("dp", "mp"),
        P("dp", "mp"),
        P("mp", "dp"),
        P("dp", "mp"),
        P("mp", "dp"),
    )
    return jax.shard_map(shards, mesh=mesh, in_specs=in_specs, out_specs=out_specs, check_vma=False)
```

```python
import functools
import math

import jax
import jax.numpy as jnp
from jax import lax
from jax.experimental import pallas as pl
from jax.experimental.pallas import tpu as pltpu
from jax.sharding import PartitionSpec as P

MESH = pl.DeviceIdType.MESH
bf16, f32 = jnp.bfloat16, jnp.float32
CAND = 16
D, HEAD, HEADS = 768, 64, 12
PER = HEADS // 4
WIDE = PER * HEAD
WIN = 8
COLS = HEADS * WIN
TILE = 256
eps = 1e-6
FAR = -1e30
VMEM = 253 << 18
UNROLL = 5
OUTS = 2


def dot(a, b, ca=1, cb=0):
    return lax.dot_general(a, b, (((ca,), (cb,)), ((), ())), preferred_element_type=f32)


def exact(a, b):
    return lax.dot_general(a, b, (((1,), (0,)), ((), ())), preferred_element_type=f32, precision=lax.Precision.HIGHEST)


def iota(shape, axis):
    return lax.broadcasted_iota(jnp.int32, shape, axis)


def to_column(row):
    k = row.shape[1]
    return jnp.sum(jnp.where(iota((k, k), 0) == iota((k, k), 1), row, 0.0), axis=1, keepdims=True)


def to_row(column):
    k = column.shape[0]
    return jnp.sum(jnp.where(iota((k, k), 0) == iota((k, k), 1), column, 0.0), axis=0, keepdims=True)


def fold_row(row):
    parts = [row[:, k * 128:(k + 1) * 128] for k in range(D // 128)]
    return jnp.concatenate(parts + [jnp.zeros((8 - D // 128, 128), f32)], axis=0)


def unfold_row(x):
    return jnp.concatenate([x[k:k + 1] for k in range(D // 128)], axis=1)


def rms(v):
    r = lax.rsqrt(jnp.mean(v * v, axis=-1, keepdims=True) + eps)
    return v * r, r


def norm_back(y, r, pushed):
    return r * (pushed - y * jnp.mean(pushed * y, axis=-1, keepdims=True))


def gelu(u):
    c = math.sqrt(2.0 / math.pi)
    t = jnp.tanh(c * (u + 0.044715 * u * u * u))
    return 0.5 * u * (1.0 + t), 0.5 * (1.0 + t) + 0.5 * u * (1.0 - t * t) * c * (1.0 + 3 * 0.044715 * u * u)


def expand(x):
    col = iota(x.shape, 1) // HEAD
    return jnp.concatenate([jnp.where(col == j, x, 0) for j in range(PER)], axis=0)


def collapse(x, rows):
    out = 0
    for j in range(PER):
        part = x[j * rows:(j + 1) * rows]
        out = out + jnp.where(iota(part.shape, 1) // HEAD == j, part, 0)
    return out


def per_head(x, m, rows):
    col = iota((rows, WIDE), 1) // HEAD
    out = jnp.where(col == 0, x[:, PER * m:PER * m + 1], 0)
    for j in range(1, PER):
        out = jnp.where(col == j, x[:, PER * m + j:PER * m + j + 1], out)
    return out


def to_pairs(x):
    n = x.shape[0]
    wide = jnp.broadcast_to(x[:, None, :], (n, WIN, 128)).reshape(n * WIN, 128)
    wide = jnp.where(iota(wide.shape, 1) % WIN == iota(wide.shape, 0) % WIN, wide, 0.0)
    return exact(wide, (iota((128, 128), 0) // WIN == iota((128, 128), 1)).astype(f32))


def to_windows(x):
    wide = exact(x, (iota((128, 128), 0) == iota((128, 128), 1) // WIN).astype(f32))
    wide = jnp.where(iota(wide.shape, 1) % WIN == iota(wide.shape, 0) % WIN, wide, 0.0)
    return jnp.sum(wide.reshape(-1, WIN, 128), axis=1)


def put(src, dst, ssem, rsem, where):
    return pltpu.make_async_remote_copy(src_ref=src, dst_ref=dst, send_sem=ssem, recv_sem=rsem, device_id=where, device_id_type=MESH)


def flips(m):
    return (m + 2) % 4, m + 1 - 2 * (m % 2)


def merge(ca, la, cb, lb):
    top = jnp.maximum(la, lb)
    ea, eb = jnp.exp(la - top), jnp.exp(lb - top)
    total = ea + eb
    wa, wb = ea / total, eb / total
    n = la.shape[0]
    return [ca[m].astype(f32) * per_head(wa, m, n) + cb[m].astype(f32) * per_head(wb, m, n) for m in range(4)], top + jnp.log(total)


def blocks(ref):
    return [ref[m // 2, :, WIDE * (m % 2):WIDE * (m % 2 + 1)] for m in range(4)]


def fill(ref, values):
    for m in range(4):
        ref[m // 2, :, WIDE * (m % 2):WIDE * (m % 2 + 1)] = values[m].astype(ref.dtype)


def loop(first, end, body):
    whole = (end - first) // UNROLL

    def some(j, _):
        for i in range(UNROLL):
            body(first + j * UNROLL + i)
        return 0

    lax.fori_loop(0, whole, some, 0)
    for k in range(first + whole * UNROLL, end):
        body(k)


class Spread:
    def __init__(self, dst, sems, wide=False, early=False):
        self.dst, self.wide, self.early = dst, wide, early
        self.groups = dst.shape[1] if wide else dst.shape[0]
        self.lines = self.groups // 2
        self.snd, self.rz, self.ry, self.rx, self.rc, self.rq = (tuple(sems) + (None,) * 4)[:6]
        self.d, self.m = lax.axis_index("dp"), lax.axis_index("mp")
        self.o, self.i = self.d // 2, self.d % 2
        self.dy = self.d + 1 - 2 * self.i
        self.xm, self.cm = flips(self.m)

    def near(self, k):
        return (self.o + self.lines - k) % self.lines * 2 + self.i

    def far(self, k):
        return (self.o + self.lines - k) % self.lines * 2 + 1 - self.i

    def at(self, mm, dd):
        return self.dst.at[mm, dd] if self.wide else self.dst.at[dd]

    def send(self, mm, dd, way, sem, where):
        put(self.at(mm, dd), self.at(mm, dd), self.snd.at[way], sem, where).start()

    def got(self, mm, dd, sem):
        put(self.at(mm, dd), self.at(mm, dd), self.snd.at[0], sem, (self.d, self.xm)).wait_recv()

    def over(self, mm, k, sems):
        self.send(mm, self.near(k), 1, sems.at[k], (self.dy, self.m))

    def mates(self, dd, j):
        if self.wide:
            if j is not None:
                self.send(self.m, dd, 2, self.rx.at[j], (self.d, self.xm))
            self.send(self.m, dd, 3, self.rc.at[0], (self.d, self.cm))

    def own(self):
        for k in range(1, self.lines):
            self.send(self.m, self.d, 0, self.rz.at[k], ((self.o + k) % self.lines * 2 + self.i, self.m))
        self.over(self.m, 0, self.ry)
        self.mates(self.d, 0)

    def arrive(self, k):
        dd = self.near(k)
        self.got(self.m, dd, self.rz.at[k])
        if self.early:
            self.mates(dd, k)
            self.over(self.m, k, self.ry)
        else:
            self.over(self.m, k, self.ry)
            self.mates(dd, k)

    def across(self, k):
        dd = self.far(k)
        self.got(self.m, dd, self.ry.at[k])
        self.mates(dd, None if self.early else self.lines + k)

    def relay(self, j):
        dd = self.near(j) if j < self.lines else self.far(j - self.lines)
        self.got(self.xm, dd, self.rx.at[j])
        self.send(self.xm, dd, 4, self.rc.at[1], (self.d, self.cm))
        if self.early:
            self.over(self.xm, j, self.rq)

    def around(self, k):
        dd = self.far(k)
        self.got(self.xm, dd, self.rq.at[k])
        self.send(self.xm, dd, 4, self.rc.at[1], (self.d, self.cm))

    def events(self, start, pace):
        n, do = self.lines, functools.partial
        out = [(start + pace * k, do(self.arrive, k)) for k in range(1, n)]
        out += [(start + pace * (k + 1) + 1, do(self.across, k)) for k in range(n)]
        if self.early:
            out += [(start + 2 * pace * k + 3, do(self.relay, k)) for k in range(n)]
            out += [(start + 2 * pace * (k + 1) + 5, do(self.around, k)) for k in range(n)]
        elif self.wide:
            out += [(start + 2 * pace * j + 3, do(self.relay, j)) for j in range(2 * n)]
        return out

    def close(self):
        xcm = (self.cm + 2) % 4
        for sem, mm in ((0, self.cm), (1, xcm)):
            put(self.dst.at[mm], self.dst.at[mm], self.snd.at[0], self.rc.at[sem], (self.d, self.cm)).wait_recv()

    def sent(self):
        def done(way, pieces):
            ref = self.dst.at[0, pl.ds(0, pieces)] if self.wide else self.dst.at[pl.ds(0, pieces)]
            put(ref, ref, self.snd.at[way], self.rz.at[0], (self.d, self.cm)).wait_send()
        done(0, self.lines - 1)
        done(1, self.groups if self.early else self.lines)
        if self.wide:
            done(2, self.lines if self.early else self.groups)
            done(3, self.groups)
            done(4, self.groups)


class Reduce:
    def __init__(self, r, yb, ys, z, sems):
        self.lines, self.r, self.yb, self.ys, self.z = r.shape[0] // 2, r, yb, ys, z
        self.snd, self.yrec, self.zrec = sems
        self.d, self.m = lax.axis_index("dp"), lax.axis_index("mp")
        self.o, self.i = self.d // 2, self.d % 2
        self.order = list(range(1, self.lines)) + [0]

    def fill(self, value, at=0):
        groups, rows = self.r.shape[0], self.r.shape[1]
        for g in range(groups):
            self.r[g, :, at:at + value.shape[1]] = value[g * rows:(g + 1) * rows].astype(bf16)

    def target(self, k):
        return (self.o + k) % self.lines

    def over(self, k):
        return put(self.r.at[2 * self.target(k) + 1 - self.i], self.yb.at[k], self.snd.at[0], self.yrec.at[k], (self.d + 1 - 2 * self.i, self.m))

    def straight(self, k):
        return put(self.ys.at[k], self.z.at[k - 1], self.snd.at[1], self.zrec.at[k - 1], (self.target(k) * 2 + self.i, self.m))

    def start(self):
        for k in self.order:
            self.over(k).start()

    def fold(self, k):
        self.over(k).wait_recv()
        self.ys[k] = (self.r[2 * self.target(k) + self.i].astype(f32) + self.yb[k].astype(f32)).astype(bf16)
        if k:
            self.straight(k).start()

    def events(self):
        return [functools.partial(self.fold, k) for k in self.order]

    def finish(self):
        out = self.ys[0].astype(f32)
        for k in range(1, self.lines):
            self.straight(k).wait_recv()
            out = out + self.z[k - 1].astype(f32)
        for way, ref in ((0, self.r.at[pl.ds(0, self.lines)]), (1, self.ys.at[pl.ds(0, self.lines - 1)])):
            put(ref, ref, self.snd.at[way], self.zrec.at[0], (self.d, self.m)).wait_send()
        return out


class Queue:
    def __init__(self):
        self.items, self.gaps = [], 1

    def plan(self, items, gaps):
        self.items += list(items)
        self.gaps = gaps

    def turn(self):
        for _ in range(-(-len(self.items) // max(self.gaps, 1))):
            self.items.pop(0)()
        self.gaps -= 1

    def rest(self):
        while self.items:
            self.items.pop(0)()


def layer_kernel(groups, weight, names, *refs):
    R = dict(zip(names, refs))

    class N:
        pass

    r = N()
    for key, ref in R.items():
        setattr(r, key, ref)
    micros, pairs = r.x0.shape[0], r.x0.shape[1]
    n = micros * pairs
    wins = pairs // WIN
    rows = r.sv.shape[0]
    tiles = r.enc.shape[0] // micros
    span = tiles * TILE
    steps = -(-(tiles + wins - 1) // UNROLL) * UNROLL
    total = 4 * groups
    lines = groups // 2
    d, m = lax.axis_index("dp"), lax.axis_index("mp")
    me = d * 4 + m
    xm, cm = flips(m)
    base = m * span

    for u in range(micros):
        for t in range(tiles):
            pltpu.make_async_copy(r.enc_hbm.at[u, pl.ds(base + t * TILE, TILE), :], r.enc.at[u * tiles + t], r.esem.at[u]).start()

    barrier = pltpu.get_barrier_semaphore()

    def hello(j, _):
        to = (me + j) % total
        pl.semaphore_signal(barrier, inc=1, device_id=(to // 4, to % 4), device_id_type=MESH)
        return 0

    lax.fori_loop(1, total, hello, 0)

    eye = (iota((rows, rows), 0) == iota((rows, rows), 1)).astype(bf16)

    def turned(x):
        return dot(eye, x, 1, 1).astype(bf16)

    def scaled(g, x):
        return (to_column(g.astype(f32)) * x.astype(f32)).astype(bf16)

    r.a1[m, d, :, 0:192] = scaled(r.g1[...], r.sv[...])
    r.a1[m, d, :, 192:384] = turned(r.so[...])
    r.a2[m, d, :, 0:192] = scaled(r.g2[...], r.wq[...])
    r.a2[m, d, :, 192:384] = r.wk[...]
    pl.semaphore_wait(barrier, total - 1)
    A1 = Spread(r.a1, (r.sa1, r.za1, r.ya1, r.xa1, r.ca1), wide=True)
    A2 = Spread(r.a2, (r.sa2, r.za2, r.ya2, r.xa2, r.ca2, r.qa2), wide=True, early=True)
    A3 = Spread(r.a3, (r.sa3, r.za3, r.ya3, r.xa3, r.ca3), wide=True)
    B1 = Spread(r.b1, (r.sb1, r.zb1, r.yb1))
    B2 = Spread(r.b2, (r.sb2, r.zb2, r.yb2))
    F = Spread(r.fd, (r.sf, r.zf, r.yf))
    A1.own()
    A2.own()
    r.b1[d] = scaled(r.g3[...], r.fi[...])
    r.a3[m, d, :, 0:192] = r.wv[...]
    r.a3[m, d, :, 192:384] = turned(r.co[...])
    r.b2[d] = r.fo[...]
    direction = unfold_row(r.dir1[...].astype(f32))
    own_dir = jnp.sum(jnp.where(iota((rows, D), 1) == d * rows + iota((rows, D), 0), direction, 0.0), axis=1, keepdims=True)
    r.fd[d] = fold_row(jnp.sum(own_dir * r.fo[...].astype(f32), axis=0, keepdims=True))

    starts = []
    for u in range(micros):
        at, w0 = jnp.int32(0), jnp.int32(0)
        for p in range(pairs):
            at = at + r.lens[u, 0, p]
            if p % WIN == WIN - 1:
                r.ends[u, p // WIN] = at
                w0 = w0 + jnp.where(at <= base, 1, 0)
        starts.append(jnp.minimum(w0, wins - 1))

    def stair(k, carry):
        out = []
        for u, (t, w, live, pt, pw, seen) in enumerate(carry):
            r.tk[u, k] = t
            r.wk_[u, k] = w
            r.at[u, k] = jnp.where(live == 1, base + t * TILE, -(1 << 20))
            r.keepw[u, k] = jnp.where(w == pw, 1.0, 0.0)
            r.keept[u, k] = jnp.where(t == pt, 1.0, 0.0)
            seen = [c + jnp.where(x <= i, 1, 0) for c, (x, i) in zip(seen, [(w, i) for i in range(wins)] + [(t, i) for i in range(tiles)])]
            wend, tend = r.ends[u, w], base + (t + 1) * TILE
            nt = t + jnp.where(wend >= tend, 1, 0)
            nw = w + jnp.where(wend <= tend, 1, 0)
            on = live * jnp.where(nt < tiles, 1, 0)
            out.append((jnp.where(on == 1, nt, t), jnp.minimum(jnp.where(on == 1, nw, w), wins - 1), on, t, w, seen))
        return out

    one, none = jnp.int32(1), jnp.int32(-1)
    ways = lax.fori_loop(0, steps, stair, [(jnp.int32(0), starts[u], one, none, none, [none] * (wins + tiles)) for u in range(micros)])
    for u in range(micros):
        for i in range(wins):
            r.lw[u, i] = ways[u][5][i]
        for i in range(tiles):
            r.lt[u, i] = ways[u][5][wins + i]
    lens = jnp.concatenate([r.lensv[u].astype(f32) for u in range(micros)] + [jnp.zeros((8 - micros, pairs), f32)], axis=0)
    for w in range(wins):
        lane = iota((pairs, 128), 1)
        pair = WIN * w + lane % WIN
        stop = exact(lens, ((iota((pairs, 128), 0) <= pair) & (lane < COLS)).astype(f32))
        start = exact(lens, ((iota((pairs, 128), 0) < pair) & (lane < COLS)).astype(f32))
        for u in range(micros):
            r.hi[u, w] = stop[u:u + 1]
            r.lo[u, w] = start[u:u + 1]

    everyone = groups * pairs
    for g in range(groups):
        r.slotr[g:g + 1, :] = jnp.concatenate([r.slot[u:u + 1, g * pairs:(g + 1) * pairs] + u * everyone for u in range(micros)], axis=1)
    square = iota((n, n), 0) == iota((n, n), 1)
    slotc = jnp.sum(jnp.where(square, r.slotr[pl.ds(d, 1), :], 0), axis=1, keepdims=True)
    keyc = slotc // CAND

    for u in range(micros):
        part = r.enc.at[pl.ds(u * tiles, tiles)]
        pltpu.make_async_copy(part, part, r.esem.at[u]).wait()

    urgent = A1.events(2.0, 1.5) + A2.events(3.5, 1.5)
    last_one = max(t for t, _ in urgent)
    later = [(5.0, A3.own), (8.0, F.own), (9.0, B1.own)] + A3.events(9.0, 2.0)
    later += [(14.0 + 2.0 * k, functools.partial(part.arrive, k)) for part in (F, B1) for k in range(1, lines)]
    events = sorted(urgent + later, key=lambda e: e[0])
    for t, e in events:
        if t <= last_one:
            e()
    A1.close()
    A2.close()
    queue = Queue()
    queue.plan([e for t, e in events if t > last_one], 6)

    def weight_of(ref, k, c0):
        return ref[k, :, :, c0:c0 + WIDE].reshape(D, WIDE)

    G0 = Reduce(r.r0, r.yr0, r.ys0, r.z0, (r.snd0, r.yrec0, r.zrec0))
    GV = Reduce(r.r2, r.yr2, r.ys2, r.z2, (r.snd2, r.yrec2, r.zrec2))
    def halve(src, buf, mid, fin, ss, rs):
        xcm = (cm + 2) % 4
        near = [put(src.at[cm], buf.at[0], ss.at[0], rs.at[0], (d, cm)), put(src.at[xcm], buf.at[1], ss.at[1], rs.at[1], (d, cm))]
        far = put(mid, fin, ss.at[2], rs.at[2], (d, xm))

        def one():
            for c in near:
                c.start()

        def two():
            for c in near:
                c.wait()
            mid[...] = (src[xm].astype(f32) + buf[1].astype(f32)).astype(bf16)
            far.start()

        def three():
            far.wait()
            return src[m].astype(f32) + buf[0].astype(f32) + fin[...].astype(f32)

        return one, two, three

    middle = steps // (2 * UNROLL) * UNROLL

    def sweep(*bodies):
        for a, b in ((0, middle), (middle, steps)):
            loop(a, b, lambda k: [body(k) for body in bodies])
            queue.turn()

    def attention(chain):
        r.chain = chain
        x0 = r.x0[...].reshape(n, D).astype(f32)
        y1b = rms(x0)[0].astype(bf16)
        x1 = x0
        for k in range(4):
            v1 = dot(y1b, weight_of(r.a1, k, 0)).astype(bf16)
            r.v1[k] = v1
            x1 = x1 + dot(v1, weight_of(r.a1, k, 192), 1, 1)
        r.x1[...] = x1
        y2b = rms(x1)[0].astype(bf16)

        def fill_windows(k, value):
            for j in range(PER):
                h = PER * k + j
                r.chain[0:micros * wins, h * WIN:(h + 1) * WIN, :] = value[j * n:(j + 1) * n].reshape(micros * wins, WIN, D)

        gap = jnp.zeros((micros, wins, 128 - COLS, D), bf16)
        for k in range(4):
            q = dot(y2b, weight_of(r.a2, k, 0)).astype(bf16)
            r.q[k] = q
            fill_windows(k, dot(expand(q), weight_of(r.a2, k, 192), 1, 1))
        r.qu[:, :, 0:COLS, :] = r.chain[0:micros * wins].astype(bf16).reshape(micros, wins, COLS, D)
        r.qu[:, :, COLS:128, :] = gap
        r.qu[:, :, 128 + COLS:256, :] = gap

        def tile_rows(u, k):
            return r.enc[u * tiles + r.tk[u, k]]

        line = iota((TILE, 128), 0).astype(f32)

        def scores(u, k):
            w = r.wk_[u, k]
            s = dot(tile_rows(u, k), r.qu[u, w, 0:128, :], 1, 1)
            at = line + r.at[u, k].astype(f32)
            s = jnp.where((at >= r.lo[u, w]) & (at < r.hi[u, w]), s, FAR)
            high = s.astype(bf16)
            r.ds[u, k] = high
            r.pa[u, k] = (s - high.astype(f32)).astype(bf16)
            r.sm[u, k] = jnp.max(s, axis=0, keepdims=True)

        def weights(u, k):
            w = r.wk_[u, k]
            s = r.ds[u, k].astype(f32) + r.pa[u, k].astype(f32)
            p = jnp.where(s > 0.5 * FAR, jnp.exp(s - r.mw[u, w]), 0.0)
            r.sm[u, k] = jnp.sum(p, axis=0, keepdims=True)
            low = p.astype(bf16)
            r.pa[u, k] = low
            r.chain[k + 1] = dot(low, tile_rows(u, k), 0, 0)[0:COLS] + r.chain[k] * r.keepw[u, k]

        def per_window(u, out, start, join):
            for w in range(wins):
                value = jnp.full((1, 128), start, f32)
                for k in range(steps):
                    value = jnp.where(jnp.full((1, 128), r.wk_[u, k]) == w, join(value, r.sm[u, k]), value)
                out[u, w] = value

        def last_of(u, keep, scale):
            for h in range(HEADS):
                parts = []
                for w in range(wins):
                    part = r.chain[r.lw[u, w] + 1, h * WIN:(h + 1) * WIN, :]
                    here = keep[w * WIN:(w + 1) * WIN, h:h + 1]
                    if scale is not None:
                        part = part * scale[w * WIN:(w + 1) * WIN, h:h + 1]
                    parts.append(jnp.where(here > 0.0, part, 0.0))
                r.c[h, u * pairs:(u + 1) * pairs, :] = jnp.concatenate(parts, axis=0).astype(bf16)

        def of(fn, u):
            return functools.partial(fn, u)

        def contexts(u):
            per_window(u, r.lw_, 0.0, jnp.add)
            tot = to_pairs(r.lw_[u].reshape(wins, 128))
            last_of(u, tot, jnp.where(tot > 0.0, 1.0 / jnp.where(tot > 0.0, tot, 1.0), 0.0))

        sweep(of(scores, 0))
        for u in range(micros):
            per_window(u, r.mw, FAR, jnp.maximum)
            r.chain[0] = jnp.zeros((COLS, D), f32)
            sweep(of(weights, u), *([of(scores, u + 1)] if u + 1 < micros else []))
            if u + 1 == micros:
                B2.own()
            contexts(u)
        queue.rest()
        A3.close()
        mx = to_pairs(r.mw[...].reshape(micros * wins, 128))
        lx = to_pairs(r.lw_[...].reshape(micros * wins, 128))
        some = lx
        lse_own = jnp.where(lx > 0.0, mx + jnp.log(jnp.where(lx > 0.0, lx, 1.0)), FAR)
        r.mx[...] = mx
        r.lown[...] = lse_own
        r.lmid[0] = lse_own.T[0:16]
        own = []
        for k in range(4):
            ctx = collapse(dot(r.c[PER * k:PER * (k + 1)].reshape(PER * n, D), weight_of(r.a3, k, 0)), n)
            own.append(ctx)
        fill(r.csend, own)
        def wide(ref):
            return jnp.concatenate([ref[...], jnp.zeros((128 - 16, n), f32)], axis=0).T

        hop = [put(r.csend, r.cbuf0, r.csem.at[0], r.crec.at[0], (d, cm)), put(r.lmid.at[0], r.lbuf0, r.csem.at[1], r.crec.at[1], (d, cm))]
        for c in hop:
            c.start()
        for k in range(lines):
            F.across(k)
        fd = r.fd[0]
        for g in range(1, groups):
            fd = fd + r.fd[g]
        fd = unfold_row(fd)
        for c in hop:
            c.wait()
        both, lse = merge(own, lse_own, blocks(r.cbuf0), wide(r.lbuf0))
        fill(r.cmid, both)
        r.lmid[1] = lse.T[0:16]
        hop = [put(r.cmid, r.cbuf1, r.csem.at[2], r.crec.at[2], (d, xm)), put(r.lmid.at[1], r.lbuf1, r.csem.at[3], r.crec.at[3], (d, xm))]
        for c in hop:
            c.start()
        for c in hop:
            c.wait()
        both, lse = merge(both, lse, blocks(r.cbuf1), wide(r.lbuf1))
        r.lse[...] = lse
        x2 = r.x1[...]
        for k in range(4):
            low = both[k].astype(bf16)
            r.ctx[k] = low
            x2 = x2 + dot(low, weight_of(r.a3, k, 192), 1, 1)
        for k in range(lines):
            B1.across(k)
        ffi = r.b1[...].reshape(D, D)
        y3, r3 = rms(x2)
        y3b = y3.astype(bf16)
        act, slope = gelu(dot(y3b, ffi))
        hid = act.astype(bf16)
        hidf = hid.astype(f32)
        score = jnp.sum(hidf * fd, axis=1, keepdims=True) + jnp.where(m == 0, jnp.sum(x2 * direction, axis=1, keepdims=True), 0.0)
        rel = jnp.concatenate([r.rel[u:u + 1, :] for u in range(micros)], axis=1)
        which = iota((8, n), 0)
        r.msgs[0] = jnp.where(which == 0, to_row(score), jnp.where(which == 1, rel, 0.0))

        def tell(j, _):
            to = (me + j) % total
            put(r.msgs.at[0], r.msgs.at[total - j], r.msem.at[0], r.msem.at[1], (to // 4, to % 4)).start()
            return 0

        lax.fori_loop(1, total, tell, 0)
        r.hid[...] = hid
        for k in range(1, lines):
            B2.arrive(k)
        r.x3[...] = x2.reshape(micros, pairs, D)

        heard = r.msgs.at[pl.ds(1, total - 1)]
        put(heard, heard, r.msem.at[0], r.msem.at[1], (d, cm)).wait()
        lane = iota((1, n), 1)

        def rows_of(g):
            four = [r.msgs[(4 * g + k - me + total) % total] for k in range(4)]
            s = (four[0] + four[1] + four[2] + four[3])[0:1]
            slot = (lane // pairs) * everyone + g * pairs + lane % pairs
            mine = r.slotr[pl.ds(g, 1), :]
            return s, four[0][1:2], mine // CAND == keyc, mine == slotc, slot // CAND == keyc, slot == slotc

        def tops(g, carry):
            a, b, own, rown = carry
            s, rel, same, mine, rsame, rmine = rows_of(g)
            return (jnp.maximum(a, jnp.where(same, s, FAR)), jnp.maximum(b, jnp.where(rsame, rel, FAR)),
                    own + jnp.where(mine, s, 0.0), rown + jnp.where(rmine, rel, 0.0))

        z = jnp.zeros((n, n), f32)
        far = jnp.full((n, n), FAR, f32)
        a, b, sown, rown = lax.fori_loop(0, groups, tops, (far, far, z, z), unroll=groups <= 8)
        a, b = jnp.max(a, axis=1, keepdims=True), jnp.max(b, axis=1, keepdims=True)
        sown, rown = jnp.sum(sown, axis=1, keepdims=True), jnp.sum(rown, axis=1, keepdims=True)

        def sums(g, carry):
            s, rel, same, _, rsame, _ = rows_of(g)
            return (carry[0] + jnp.where(same, jnp.exp(s - a), 0.0), carry[1] + jnp.where(rsame, jnp.exp(rel - b), 0.0))

        sa, sb = lax.fori_loop(0, groups, sums, (z, z), unroll=groups <= 8)
        dscore = weight * (jnp.exp(sown - a) / jnp.sum(sa, axis=1, keepdims=True) - jnp.exp(rown - b) / jnp.sum(sb, axis=1, keepdims=True))
        du = (slope * dscore * fd).astype(bf16)
        dn3p = dot(du, ffi, 1, 1)
        r.nmid[0] = dn3p.astype(bf16)
        nhop = put(r.nmid.at[0], r.nbuf.at[0], r.nsem.at[0], r.nrec.at[0], (d, cm))
        nhop.start()
        r.hsum[0] = fold_row(jnp.sum(hidf * dscore, axis=0, keepdims=True))

        def scatter(j, _):
            to = (d + j) % groups
            put(r.hsum.at[0], r.hsum.at[groups - j], r.hsem.at[0], r.hsem.at[1], (to, m)).start()
            return 0

        nhop.wait()
        part = dn3p + r.nbuf[0].astype(f32)
        r.nmid[1] = part.astype(bf16)
        nhop = put(r.nmid.at[1], r.nbuf.at[1], r.nsem.at[1], r.nrec.at[1], (d, xm))
        nhop.start()
        lax.fori_loop(1, groups, scatter, 0)
        G0.fill(dot(y3b, du, 0, 0))
        G0.start()
        nhop.wait()
        dn3 = part + r.nbuf[1].astype(f32)
        dx2 = dscore * direction + norm_back(y3, r3, dn3)
        r.dx2[...] = dx2
        gc = dx2.astype(bf16)
        delta = jnp.zeros((n, 128), f32)
        for k in range(4):
            dctx = dot(gc, weight_of(r.a3, k, 192)).astype(bf16)
            r.dctx[k] = dctx
            pick = (iota((WIDE, 128), 0) // HEAD + PER * k == iota((WIDE, 128), 1)).astype(f32)
            delta = delta + exact(dctx.astype(f32) * both[k], pick)
        ones = jnp.ones((n, 64), bf16)
        GV.fill(jnp.concatenate([dot(gc, r.ctx[m], 0, 0), dot((dn3 * y3).astype(bf16), ones, 0, 0)], axis=1))
        r.alpha[...] = to_windows(jnp.exp(jnp.minimum(r.mx[...] - lse, 1.0))).reshape(r.alpha.shape)
        r.delta[...] = to_windows(delta).reshape(r.delta.shape)
        share = jnp.exp(jnp.minimum(r.lown[...] - lse, 1.0))
        for k in range(4):
            dctx = expand(r.dctx[k])
            fill_windows(k, dot(dctx, weight_of(r.a3, k, 0), 1, 1))
            spread = jnp.concatenate([dctx[j * n:(j + 1) * n] * share[:, PER * k + j:PER * k + j + 1].astype(bf16) for j in range(PER)], axis=0)
            r.g[k] = dot(r.c[PER * k:PER * (k + 1)].reshape(PER * n, D), spread, 0, 0).astype(bf16)
        r.qu[:, :, 128:128 + COLS, :] = r.chain[0:micros * wins].astype(bf16).reshape(micros, wins, COLS, D)

        v_one, v_two, v_three = halve(r.g, r.gvb, r.gvm, r.gvf, r.vsem, r.vrec)
        v_one()

        def value_out():
            GV.fill(jnp.concatenate([v_three(), jnp.zeros((D, 64), f32)], axis=1), 256)
            GV.start()

        queue.plan([v_two] + G0.events() + [value_out] + GV.events(), 8)

        def slopes(u, k):
            w = r.wk_[u, k]
            da = dot(tile_rows(u, k), r.qu[u, w, 128:256, :], 1, 1)
            a = r.pa[u, k].astype(f32) * r.alpha[u, w]
            r.ds[u, k] = (a * (da - r.delta[u, w])).astype(bf16)

        def sums_of(u, k):
            r.chain[k + 1] = dot(r.ds[u, k], tile_rows(u, k), 0, 0)[0:COLS] + r.chain[k] * r.keepw[u, k]

        sweep(of(slopes, 0))
        for u in range(micros):
            r.chain[0] = jnp.zeros((COLS, D), f32)
            sweep(of(sums_of, u), *([of(slopes, u + 1)] if u + 1 < micros else []))
            last_of(u, some[u * pairs:(u + 1) * pairs], None)

    pl.run_scoped(attention, pltpu.VMEM((steps + 1, COLS, D), f32))

    def rest_of_it(r1, ys1, r3, ys3, full, out):
        r.r1, r.ys1, r.r3, r.ys3, r.full, r.out = r1, ys1, r3, ys3, full, out
        G1 = Reduce(r.r1, r.yr1, r.ys1, r.z1, (r.snd1, r.yrec1, r.zrec1))
        GK = Reduce(r.r3, r.yr3, r.ys3, r.z3, (r.snd3, r.yrec3, r.zrec3))
        part = [collapse(dot(r.c[PER * k:PER * (k + 1)].reshape(PER * n, D), weight_of(r.a2, k, 192)), n) for k in range(4)]
        fill(r.csend, part)
        hop = put(r.csend, r.cbuf0, r.qsem.at[0], r.qrec.at[0], (d, cm))
        hop.start()
        for k in range(4):
            r.g[k] = dot(r.c[PER * k:PER * (k + 1)].reshape(PER * n, D), expand(r.q[k]), 0, 0).astype(bf16)
        k_one, k_two, k_three = halve(r.g, r.gkb, r.gvm, r.gkf, r.ksem, r.krec)
        hop.wait()
        part = [x + y.astype(f32) for x, y in zip(part, blocks(r.cbuf0))]
        fill(r.cmid, part)
        hop = put(r.cmid, r.cbuf1, r.qsem.at[1], r.qrec.at[1], (d, xm))
        hop.start()
        k_one()
        queue.rest()
        for k in range(lines):
            B2.across(k)
        x3p = dot(r.hid[...], r.b2[...].reshape(D, D), 1, 1)
        r.nmid[0] = x3p.astype(bf16)
        xhop = put(r.nmid.at[0], r.nbuf.at[0], r.xsem.at[0], r.xrec.at[0], (d, cm))
        xhop.start()
        x1 = r.x1[...]
        y1, g1 = rms(r.x0[...].reshape(n, D).astype(f32))
        y2, g2 = rms(x1)
        k_two()
        hop.wait()
        dn2 = 0
        for k in range(4):
            dq = (part[k] + blocks(r.cbuf1)[k].astype(f32)).astype(bf16)
            r.dq[k] = dq
            dn2 = dn2 + dot(dq, weight_of(r.a2, k, 0), 1, 1)
        dx1 = r.dx2[...] + norm_back(y2, g2, dn2)
        gs = dx1.astype(bf16)
        dn1 = 0
        for k in range(4):
            dv = dot(gs, weight_of(r.a1, k, 192)).astype(bf16)
            r.dctx[k] = dv
            dn1 = dn1 + dot(dv, weight_of(r.a1, k, 0), 1, 1)
        r.dx0[...] = (dx1 + norm_back(y1, g1, dn1)).reshape(micros, pairs, D)
        ones = jnp.ones((n, 64), bf16)
        half_ones = jnp.where(iota((n, 64), 1) < 32, ones, 0)
        small = [dot(y1.astype(bf16), r.dctx[m], 0, 0), dot(gs, r.v1[m], 0, 0), dot(y2.astype(bf16), r.dq[m], 0, 0)]
        tail = dot((dn1 * y1).astype(bf16), half_ones, 0, 0) + dot((dn2 * y2).astype(bf16), ones - half_ones, 0, 0)
        G1.fill(jnp.concatenate(small + [tail], axis=1))
        G1.start()
        GK.fill(jnp.concatenate([k_three(), jnp.zeros((D, 64), f32)], axis=1))
        GK.start()
        xhop.wait()
        x3p = x3p + r.nbuf[0].astype(f32)
        r.nmid[1] = x3p.astype(bf16)
        xhop = put(r.nmid.at[1], r.nbuf.at[1], r.xsem.at[1], r.xrec.at[1], (d, xm))
        xhop.start()
        queue.plan(G1.events() + GK.events(), micros * 2)

        def rows_out(u, t, slot):
            return pltpu.make_async_copy(r.out.at[slot], r.de.at[u, pl.ds(t * TILE, TILE), :], r.osem.at[slot])

        for u in range(micros):
            if u == 0:
                r.full[...] = jnp.zeros_like(r.full)
            loop(0, steps, functools.partial(place, r, u))
            queue.turn()
            for t in range(tiles):
                slot = (u * tiles + t) % OUTS
                if u * tiles + t >= OUTS:
                    rows_out(u, t, slot).wait()
                k = jnp.maximum(r.lt[u, t], 0)
                r.out[slot] = r.enc[k]
                rows_out(u, t, slot).start()
                if t % 6 == 5:
                    queue.turn()
        for slot in range(OUTS):
            rows_out(micros - 1, tiles - 1, slot).wait()
        queue.rest()

        heard = r.hsum.at[pl.ds(1, groups - 1)]
        put(heard, heard, r.hsem.at[0], r.hsem.at[1], (d, cm)).wait()
        total_h = r.hsum[0]
        for g in range(1, groups):
            total_h = total_h + r.hsum[g]
        r.hs[...] = total_h
        xhop.wait()
        r.x3[...] = r.x3[...] + (x3p + r.nbuf[1].astype(f32)).reshape(micros, pairs, D)
        r.out0[...] = G0.finish()
        r.out2[...] = GV.finish()
        r.out1[...] = G1.finish()
        r.out3[...] = GK.finish()

    pl.run_scoped(rest_of_it, pltpu.VMEM((groups, rows, 640), bf16), pltpu.VMEM((lines, rows, 640), bf16),
                  pltpu.VMEM((groups, rows, 256), bf16), pltpu.VMEM((lines, rows, 256), bf16), pltpu.VMEM((TILE, D), f32), pltpu.VMEM((OUTS, TILE, D), bf16))
    for part in (A1, A2, A3, B1, B2, F):
        part.sent()


def place(r, u, k):
    w = r.wk_[u, k]
    a = (r.pa[u, k].astype(f32) * r.alpha[u, w]).astype(bf16)
    acc = dot(jnp.concatenate([r.ds[u, k], a], axis=1), r.qu[u, w]) + r.full[...] * r.keept[u, k]
    r.full[...] = acc
    r.enc[k] = acc.astype(bf16)


def layer(groups, weight, x0, encoded, lens, slot, rel, dir1, g1, g2, g3, sv, so, wq, wk, wv, co, fi, fo):
    micros, pairs = x0.shape[0], x0.shape[1]
    n, wins, rows, lines = micros * pairs, pairs // WIN, sv.shape[0], groups // 2
    span = encoded.shape[1] // 4
    tiles = span // TILE
    steps = -(-(tiles + wins - 1) // UNROLL) * UNROLL
    sd = jax.ShapeDtypeStruct
    any_, vm, sm = (pl.BlockSpec(memory_space=s) for s in (pl.ANY, pltpu.VMEM, pltpu.SMEM))
    S, V, M = pltpu.SemaphoreType.DMA, pltpu.VMEM, pltpu.SMEM
    ins = dict(x0=x0, enc_hbm=encoded, lens=lens, lensv=lens, slot=slot, rel=rel, dir1=dir1, g1=g1, g2=g2, g3=g3,
               sv=sv, so=so, wq=wq, wk=wk, wv=wv, co=co, fi=fi, fo=fo)
    places = dict(enc_hbm=any_, lens=sm)
    outs = dict(x3=sd((micros, pairs, D), f32), dx0=sd((micros, pairs, D), f32), de=sd((micros, span, D), bf16), hs=sd((8, 128), f32),
                out0=sd((rows, D), f32), out1=sd((rows, 640), f32), out2=sd((rows, 512), f32), out3=sd((rows, 256), f32))
    places.update(de=any_)
    scratch = dict(
        enc=V((max(micros * tiles, steps), TILE, D), bf16), esem=S((micros,)),
        a1=V((4, groups, rows, 384), bf16), a2=V((4, groups, rows, 384), bf16), a3=V((4, groups, rows, 384), bf16),
        b1=V((groups, rows, D), bf16), b2=V((groups, rows, D), bf16), fd=V((groups, 8, 128), f32), hid=V((n, D), bf16),
        ends=M((micros, wins), jnp.int32), tk=M((micros, steps), jnp.int32), wk_=M((micros, steps), jnp.int32), at=M((micros, steps), jnp.int32),
        keepw=M((micros, steps), f32), keept=M((micros, steps), f32), lw=M((micros, wins), jnp.int32), lt=M((micros, tiles), jnp.int32),
        lo=V((micros, wins, 1, 128), f32), hi=V((micros, wins, 1, 128), f32), slotr=V((groups, n), jnp.int32),
        x1=V((n, D), f32), v1=V((4, n, WIDE), bf16), q=V((4, n, WIDE), bf16), qu=V((micros, wins, 256, D), bf16), sm=V((micros, steps, 1, 128), f32), mw=V((micros, wins, 1, 128), f32), lw_=V((micros, wins, 1, 128), f32),
        ds=V((micros, steps, TILE, 128), bf16), pa=V((micros, steps, TILE, 128), bf16), c=V((HEADS, n, D), bf16), mx=V((n, 128), f32), lown=V((n, 128), f32), lse=V((n, 128), f32),
        csend=V((2, n, 384), bf16), cmid=V((2, n, 384), bf16), cbuf0=V((2, n, 384), bf16), cbuf1=V((2, n, 384), bf16), lmid=V((2, 16, n), f32), lbuf0=V((16, n), f32), lbuf1=V((16, n), f32),
        csem=S((4,)), crec=S((4,)), ctx=V((4, n, WIDE), bf16), msgs=V((4 * groups, 8, n), f32), msem=S((2,)),
        xsem=S((2,)), xrec=S((2,)), nmid=V((2, n, D), bf16), nbuf=V((2, n, D), bf16), nsem=S((2,)), nrec=S((2,)),
        hsum=V((groups, 8, 128), f32), hsem=S((2,)), dx2=V((n, D), f32), dctx=V((4, n, WIDE), bf16), dq=V((4, n, WIDE), bf16),
        alpha=V((micros, wins, 1, 128), f32), delta=V((micros, wins, 1, 128), f32),
        g=V((4, D, WIDE), bf16), gvb=V((2, D, WIDE), bf16), gvm=V((D, WIDE), bf16), gvf=V((D, WIDE), bf16), vsem=S((3,)), vrec=S((3,)),
        gkb=V((2, D, WIDE), bf16), gkf=V((D, WIDE), bf16), ksem=S((3,)), krec=S((3,)), qsem=S((2,)), qrec=S((2,)),
        osem=S((OUTS,)),
    )
    for part in ("a1", "a2", "a3", "b1", "b2", "f"):
        scratch.update({"s" + part: S((5,)), "z" + part: S((lines,)), "y" + part: S((lines,))})
        if part[0] == "a":
            scratch.update({"x" + part: S((groups,)), "c" + part: S((2,)), "q" + part: S((lines,))})
    for tag, columns in (("0", 768), ("1", 640), ("2", 512), ("3", 256)):
        piece = lambda k: V((k, rows, columns), bf16)
        if tag in "02":
            scratch.update({"r" + tag: piece(groups), "ys" + tag: piece(lines)})
        scratch.update({"yr" + tag: piece(lines), "z" + tag: piece(lines - 1),
                        "snd" + tag: S((2,)), "yrec" + tag: S((lines,)), "zrec" + tag: S((lines - 1,))})
    names = tuple(ins) + tuple(outs) + tuple(scratch)
    return pl.pallas_call(
        functools.partial(layer_kernel, groups, weight, names),
        out_shape=tuple(outs.values()),
        in_specs=[places.get(k, vm) for k in ins], out_specs=[places.get(k, vm) for k in outs],
        scratch_shapes=list(scratch.values()),
        compiler_params=pltpu.CompilerParams(collective_id=0, has_side_effects=True, vmem_limit_bytes=VMEM),
        name="decoder_layer",
    )(*ins.values())


def outputs_kernel(count, dir_ref, g1, g2, g3, *refs):
    sums, de = refs[:7], refs[7]
    outs, de_out = refs[8:21], refs[21]
    hs, out0, out1, out2, out3 = refs[22:27]
    made, (room, sem, hsem, osem) = refs[27:40], refs[40:]
    (g_self, g_cross, g_ff, self_value, self_out, query, key, value, cross_out, ff_in, ff_out, x3_out, dx0_out) = made
    leave = [pltpu.make_async_copy(src, dst, osem.at[k]) for k, (src, dst) in enumerate(zip(made, outs))]
    near = [pltpu.make_async_copy(src, dst, hsem.at[k]) for k, (src, dst) in enumerate(zip(sums, (hs, out0, out1, out2, out3, x3_out, dx0_out)))]
    for c in near:
        c.start()
    height = room.shape[1]
    parts = de.shape[1] // height
    every = [(u, pl.ds(k * height, height), u * parts + k) for u in range(de.shape[0]) for k in range(parts)]
    loads = [pltpu.make_async_copy(de.at[u, at], room.at[k], sem.at[0, k]) for u, at, k in every]
    stores = [pltpu.make_async_copy(room.at[k], de_out.at[u, at], sem.at[1, k]) for u, at, k in every]
    for c in loads:
        c.start()
    rows = out0.shape[0]
    columns = [to_column(g[...].astype(f32)) for g in (g1, g2, g3)]
    mine = iota((rows, D), 1) == lax.axis_index("dp") * rows + iota((rows, D), 0)
    own_dir = jnp.sum(jnp.where(mine, unfold_row(dir_ref[...].astype(f32)), 0.0), axis=1, keepdims=True)
    for c in near:
        c.wait()
    for c, back in list(zip(loads, stores))[:count // 2]:
        c.wait()
        back.start()
    g_self[...] = to_row(out1[:, 576:577] / columns[0])
    g_cross[...] = to_row(out1[:, 608:609] / columns[1])
    g_ff[...] = to_row(out2[:, 192:193] / columns[2])
    self_value[...] = out1[:, 0:192] * columns[0]
    self_out[...] = out1[:, 192:384].T
    query[...] = out1[:, 384:576] * columns[1]
    key[...] = out3[:, 0:192]
    value[...] = out2[:, 256:448]
    cross_out[...] = out2[:, 0:192].T
    ff_in[...] = out0[...] * columns[2]
    ff_out[...] = own_dir * unfold_row(hs[...])
    for c in leave:
        c.start()
    for c, back in list(zip(loads, stores))[count // 2:]:
        c.wait()
        back.start()
    for c in stores + leave:
        c.wait()


def outputs(dir1, gains, hs, out0, out1, out2, out3, x3, dx0, de):
    rows, height = out0.shape[0], 512
    count = de.shape[0] * de.shape[1] // height
    sd = jax.ShapeDtypeStruct
    tall, flat = sd((rows, WIDE), f32), sd((WIDE, rows), f32)
    any_, vm = (pl.BlockSpec(memory_space=s) for s in (pl.ANY, pltpu.VMEM))
    shapes = (sd((1, rows), f32),) * 3 + (tall, flat, tall, tall, tall, flat, sd((rows, D), f32), sd((rows, D), f32), sd(x3.shape, f32), sd(x3.shape, f32))
    return pl.pallas_call(
        functools.partial(outputs_kernel, count),
        out_shape=shapes + (sd(de.shape, bf16),),
        in_specs=[vm] * 4 + [any_] * 8, out_specs=[any_] * 14,
        scratch_shapes=[pltpu.VMEM(x.shape, f32) for x in (hs, out0, out1, out2, out3) + shapes] +
                       [pltpu.VMEM((count, height, D), bf16), pltpu.SemaphoreType.DMA((2, count)), pltpu.SemaphoreType.DMA((7,)),
                        pltpu.SemaphoreType.DMA((len(shapes),))],
        compiler_params=pltpu.CompilerParams(vmem_limit_bytes=VMEM),
        name="outputs",
    )(dir1, *gains, hs, out0, out1, out2, out3, x3, dx0, de)


def shards(dec_in, encoded, seg_lengths, pair_slot, relevance, score_dir, gain_self, gain_cross, gain_ff,
           self_value, self_out, cross_query, cross_key, cross_value, cross_out, ff_in, ff_out):
    groups = lax.axis_size("dp")
    gains = [g.reshape(1, -1) for g in (gain_self, gain_cross, gain_ff)]
    dir1 = score_dir.reshape(D // 128, 128)
    x3, dx0, d_encoded, hs, out0, out1, out2, out3 = layer(
        groups, CAND * math.sqrt(D), dec_in, encoded, seg_lengths, pair_slot, relevance, dir1, *gains,
        self_value, self_out, cross_query, cross_key, cross_value, cross_out, ff_in, ff_out.T)
    g1, g2, g3, *weights, x3, dx0, d_encoded = outputs(dir1, gains, hs, out0, out1, out2, out3, x3, dx0, d_encoded)
    weights[-1] = weights[-1].T
    return (x3, dx0, d_encoded, g1.reshape(-1), g2.reshape(-1), g3.reshape(-1), *weights)


def solution(mesh):
    in_specs = (
        P(None, "dp", None),
        P(None, "dp", None),
        P(None, "dp", None),
        P(),
        P(None, "dp"),
        P(),
        P("dp"),
        P("dp"),
        P("dp"),
        P("dp", "mp"),
        P("mp", "dp"),
        P("dp", "mp"),
        P("dp", "mp"),
        P("dp", "mp"),
        P("mp", "dp"),
        P("dp", "mp"),
        P("mp", "dp"),
    )
    out_specs = (
        P(None, "dp", None),
        P(None, "dp", None),
        P(None, ("dp", "mp"), None),
        P("dp"),
        P("dp"),
        P("dp"),
        P("dp", "mp"),
        P("mp", "dp"),
        P("dp", "mp"),
        P("dp", "mp"),
        P("dp", "mp"),
        P("mp", "dp"),
        P("dp", "mp"),
        P("mp", "dp"),
    )
    return jax.shard_map(shards, mesh=mesh, in_specs=in_specs, out_specs=out_specs, check_vma=False)
```
